256 devices in a mesh: group: 16 (over x, z_hi, core), tp: 16 (over y, z_lo).
Axes of the slice: x: 4, y: 4, z: 8 (z_hi: 2, z_lo: 4; z = z_hi * 4 + z_lo), core: 2. Of those that a mesh axis runs over, the one named last changes fastest.
Arguments:
- states: bfloat16 [4, 1024, 5120], P(None, 'group'), may hold values from -6 to 6
- query_weight: bfloat16 [5120, 4096], P(None, 'tp'), may hold values from -0.078125 to 0.078125
- key_value_weight: bfloat16 [5120, 1024], P(None, 'tp'), may hold values from -0.078125 to 0.078125
- output_weight: bfloat16 [4096, 5120], P('tp'), may hold values from -0.09375 to 0.09375
- query_adapter_lower: bfloat16 [5120, 64], P(('group', 'tp')), may hold values from -0.078125 to 0.078125
- query_adapter_upper: bfloat16 [64, 4096], P('group', 'tp'), may hold values from -0.75 to 0.75
- output_adapter_lower: bfloat16 [64, 4096], P('group', 'tp'), may hold values from -0.09375 to 0.09375
- output_adapter_upper: bfloat16 [5120, 64], P(('group', 'tp')), may hold values from -0.75 to 0.75
- cached_key_rows: bfloat16 [1024, 4, 64, 128], P('group'), may hold values from -160 to 160
- cached_value_rows: bfloat16 [1024, 4, 64, 128], P('group'), may hold values from -6 to 6
- cached_length: int32 [1024], P('group'), may hold values from 1 to 64, as said below
Outputs:
- attn_out: bfloat16 [4, 1024, 5120], P(None, 'group', 'tp')
The draws below stay inside these ranges and needn't reach their ends.
Inputs may be any that keep to these rules, and one draw needn't show every extreme that they name: `cached_length`: some rollout has exactly 64 cached positions.
All inputs are finite; a program needn't handle non-finite values.
Results may differ from the reference program's by a relative error of at most 0.024.
The reference program's roundings to bfloat16 on the way count: a program that leaves them out, or rounds other values in their place, can miss the bound.
Values may be sent and summed in bfloat16 or wider, within the bound.
No kernel may reach another device: no remote copies, remote signals or barrier semaphores. Data moves between devices by JAX's collectives and lax.ppermute only.
A program may use at most 128 MiB of HBM per device.

```python
import jax
import jax.numpy as jnp
from jax import lax

MODEL_WIDTH = 5120
QH = 32
KVH = 4
HD = 128
ADAPTER_RANK = 64
STEPS = 4
CACHE = 64
ROLL = 1024
QUERY_WIDTH = 4096
KVW = 1024


def draw_cached_key_rows(key, part):
    key = jax.random.fold_in(key, 11)
    base = jax.random.normal(key, (ROLL, KVH, CACHE, HD), jnp.float32)
    return jnp.clip(base, -6.0, 6.0).astype(jnp.bfloat16)


def draw_cached_length(key, part):
    key = jax.random.fold_in(key, 23)
    lens = jax.random.randint(key, (ROLL,), 1, CACHE + 1)
    chosen = jax.random.randint(jax.random.fold_in(key, 2), (), 0, ROLL)
    rows = jnp.arange(ROLL, dtype=jnp.int32)
    return jnp.where(rows == chosen, CACHE, lens).astype(jnp.int32)


def block_levels(stream_key, dims, cuts, least, largest):
    level, own = 1.0, jax.random.fold_in(stream_key, 6)
    for axis_at, parts in cuts:
        heights = jnp.exp(jax.random.uniform(jax.random.fold_in(own, axis_at), (parts,), jnp.float32, least / len(cuts), largest / len(cuts)))
        level = level * jnp.repeat(heights, dims[axis_at] // parts).reshape([-1 if axis == axis_at else 1 for axis in range(len(dims))])
    return level


def noise(stream_key, dims, scale, reach, split=(), kind=jnp.bfloat16):
    drawn = scale * jax.random.normal(stream_key, dims, jnp.float32)
    if split:
        drawn = drawn * block_levels(stream_key, dims, split, -0.22, 0.18)
    return jnp.clip(drawn, -reach, reach).astype(kind)


def setup_inputs(seed: int = 0) -> dict:
    splits = jax.random.split(jax.random.key(seed), 12)
    return {
        "states": noise(splits[0], (STEPS, ROLL, MODEL_WIDTH), 1.0, 6.0, ((1, 16),)),
        "query_weight": noise(splits[1], (MODEL_WIDTH, QUERY_WIDTH), MODEL_WIDTH ** -0.5, 0.078125, ((1, 16),)),
        "key_value_weight": noise(splits[2], (MODEL_WIDTH, KVW), MODEL_WIDTH ** -0.5, 0.078125, ((1, 16),)),
        "output_weight": noise(splits[3], (QUERY_WIDTH, MODEL_WIDTH), QUERY_WIDTH ** -0.5, 0.09375, ((0, 16),)),
        "query_adapter_lower": noise(splits[4], (MODEL_WIDTH, ADAPTER_RANK), MODEL_WIDTH ** -0.5, 0.078125, ((0, 256),)),
        "query_adapter_upper": noise(splits[5], (ADAPTER_RANK, QUERY_WIDTH), ADAPTER_RANK ** -0.5, 0.75, ((0, 16), (1, 16))),
        "output_adapter_lower": noise(splits[6], (ADAPTER_RANK, QUERY_WIDTH), QUERY_WIDTH ** -0.5, 0.09375, ((0, 16), (1, 16))),
        "output_adapter_upper": noise(splits[7], (MODEL_WIDTH, ADAPTER_RANK), ADAPTER_RANK ** -0.5, 0.75, ((0, 256),)),
        "cached_key_rows": draw_cached_key_rows(jax.random.fold_in(splits[11], 71), 0),
        "cached_value_rows": noise(splits[9], (ROLL, KVH, CACHE, HD), 1.0, 6.0, ((0, 16),)),
        "cached_length": draw_cached_length(jax.random.fold_in(splits[11], 71), 0),
    }


adapter_scale = 2.0

def reference(states, query_weight, key_value_weight, output_weight, query_adapter_lower, query_adapter_upper, output_adapter_lower, output_adapter_upper, cached_key_rows, cached_value_rows, cached_length):
    combined_query_weight = (query_weight.astype(jnp.float32) + adapter_scale * jnp.dot(query_adapter_lower, query_adapter_upper, preferred_element_type=jnp.float32)).astype(jnp.bfloat16)
    output_update = lax.dot_general(output_adapter_lower, output_adapter_upper, (((0,), (1,)), ((), ())), preferred_element_type=jnp.float32)
    combined_output_weight = (output_weight.astype(jnp.float32) + adapter_scale * output_update).astype(jnp.bfloat16)
    flat = states.reshape(STEPS * ROLL, MODEL_WIDTH).astype(jnp.float32)
    normed = (flat * lax.rsqrt(lax.optimization_barrier(jnp.mean(flat * flat, axis=1, keepdims=True)) + 1e-06)).astype(jnp.bfloat16)
    queries = jnp.dot(normed, combined_query_weight, preferred_element_type=jnp.float32).astype(jnp.bfloat16)
    new_kv = jnp.dot(normed, key_value_weight, preferred_element_type=jnp.float32).astype(jnp.bfloat16)
    group_size = QH // KVH
    qf = queries.astype(jnp.float32).reshape(STEPS, ROLL, KVH, group_size, HD)
    kvf = new_kv.astype(jnp.float32).reshape(STEPS, ROLL, 2, KVH, HD)
    new_keys = kvf[:, :, 0]
    new_vals = kvf[:, :, 1]
    kc = cached_key_rows.astype(jnp.float32)
    vc = cached_value_rows.astype(jnp.float32)
    factor = 1.0 / HD ** 0.5
    score_c = jnp.einsum('srghd,rgpd->srghp', qf, kc) * factor
    positions = jnp.arange(CACHE, dtype=jnp.int32)
    mask_c = (positions[None, :] < cached_length[:, None])[None, :, None, None, :]
    score_c = jnp.where(mask_c, score_c, -1e+30)
    score_n = jnp.einsum('srghd,jrgd->srghj', qf, new_keys) * factor
    steps_idx = jnp.arange(STEPS, dtype=jnp.int32)
    mask_n = (steps_idx[None, :] <= steps_idx[:, None])[:, None, None, None, :]
    score_n = jnp.where(mask_n, score_n, -1e+30)
    scores = jnp.concatenate([score_c, score_n], axis=-1)
    top = lax.optimization_barrier(jnp.max(scores, axis=-1, keepdims=True))
    expo = jnp.exp(scores - top)
    probs = (expo / lax.optimization_barrier(jnp.sum(expo, axis=-1, keepdims=True))).astype(jnp.bfloat16).astype(jnp.float32)
    context = jnp.einsum('srghp,rgpd->srghd', probs[..., :CACHE], vc) + jnp.einsum('srghj,jrgd->srghd', probs[..., CACHE:], new_vals)
    context = context.reshape(STEPS * ROLL, QUERY_WIDTH).astype(jnp.bfloat16)
    out = jnp.dot(context, combined_output_weight, preferred_element_type=jnp.float32).astype(jnp.bfloat16)
    return out.reshape(STEPS, ROLL, MODEL_WIDTH)
```

```python
import jax
import jax.numpy as jnp
import numpy as np
from jax import lax
from jax.experimental import pallas as pl
from jax.experimental.pallas import tpu as pltpu
from jax.sharding import Mesh
from jax.sharding import PartitionSpec as P

HD = 128
STEPS = 4
ROWS = 256
WIDTH = 5120
NX, NZH, NC, NY, NZ = 4, 2, 2, 4, 4
GROUP = ("x", "zh", "c")
TP = ("y", "z")
BF = jnp.bfloat16
F32 = jnp.float32
VLIMIT = 56 * 1024 * 1024
MSG = 48
XROWS = 720

SMEM = pl.BlockSpec(memory_space=pltpu.SMEM)


def params():
    return pltpu.CompilerParams(vmem_limit_bytes=VLIMIT)


def mm(a, b):
    return jnp.dot(a, b, preferred_element_type=F32)


def mm_t(a, b):
    return lax.dot_general(a, b, (((1,), (1,)), ((), ())), preferred_element_type=F32)


def norm_kernel(states, wkv_t, blocks, kv_t, flat):
    def rows(i, carry):
        r = pl.multiple_of(i * 32, 32)
        x = states[pl.ds(r, 32), :].astype(F32)
        scale = lax.rsqrt(jnp.mean(x * x, axis=1, keepdims=True) + 1e-06)
        normed = (x * scale).astype(BF)
        flat[pl.ds(r, 32), :] = normed
        for xc in range(8):
            g = (xc // 2) * 4 + xc % 2
            blocks[xc, pl.ds(r, 32), :] = jnp.concatenate(
                [normed[:, g * 320 : g * 320 + 320], normed[:, g * 320 + 640 : g * 320 + 960]], axis=1
            )
        return carry

    lax.fori_loop(0, ROWS // 32, rows, 0)
    kv_t[...] = mm_t(flat[...], wkv_t[...]).T.astype(BF)


def sort_kernel(ids, got, out):
    i = lax.broadcasted_iota(jnp.int32, (80, 4 * MSG), 0)
    j = lax.broadcasted_iota(jnp.int32, (80, 4 * MSG), 1)
    hit = i < 0
    for p in range(4):
        hit = hit | ((j - MSG * p == i - 20 * p) & (i >= 20 * p) & (i < 20 * p + 20))
    pick = jnp.where(hit, 1.0, 0.0).astype(BF)
    for q in range(8):
        out[80 * q : 80 * q + 80, :] = mm(pick, got[4 * q : 4 * q + 4].reshape(4 * MSG, 128)).astype(BF)
    y, z = ids[3], ids[4]
    own = [got[zh * 16 + y * NZ + z, 32:48, :].astype(F32)[:8] for zh in range(2)]
    out[640:656, :] = jnp.concatenate(own, axis=0).astype(BF)
    for yy in range(NY):
        part = [got[zh * 16 + yy * NZ + z, 32:48, :].astype(F32)[8:] for zh in range(2)]
        out[656 + 16 * yy : 672 + 16 * yy, :] = jnp.concatenate(part, axis=0).astype(BF)


def rank_order(ids, half, first):
    r = lax.broadcasted_iota(jnp.int32, (128, 128), 0)
    j = lax.broadcasted_iota(jnp.int32, (128, 128), 1)
    x, c = ids[0], ids[2]
    k, o = (j >> 5) & 3, (j >> 4) & 1
    zh, h, i = (j >> 3) & 1, (j >> 2) & 1, j & 3
    xs = (x - k + 4) & 3
    rank = (xs * 4 + zh * 2 + (c + o - 2 * c * o)) * 4 + i
    return jnp.where((h == half) & (r == rank + first), 1.0, 0.0).astype(BF)


def attend_kernel(ids, head, *refs):
    blocks = refs[:8]
    wq, normed, kc, vc, kv0, kv1, kv2, kv3, lens, ctx, kv, qs, cs = refs[8:]
    x, c, z = ids[0], ids[2], ids[4]
    stack = jnp.concatenate([b[640:656, :] for b in blocks], axis=0)
    upper = jnp.concatenate(
        [2.0 * mm(rank_order(ids, h, 0), stack) for h in range(2)], axis=1
    ).astype(BF)
    total = jnp.zeros((ROWS, 256), F32)
    for k in range(4):
        for o in range(2):
            xs = (x - k + 4) & 3
            cs_ = c + o - 2 * c * o
            rank = mm(blocks[2 * k + o][0:640, :], upper)
            off = pl.multiple_of((xs * 4 + cs_) * 320, 320)
            base = jnp.concatenate([wq[pl.ds(off, 320), :], wq[pl.ds(off + 640, 320), :]], axis=0)
            merged = (base.astype(F32) + rank).astype(BF)
            total = total + mm(normed[xs * 2 + cs_], merged)
    qs[...] = total.astype(BF).astype(F32)
    for k, ref in enumerate((kv0, kv1, kv2, kv3)):
        kv[(z - k + 4) & 3] = ref[...]
    key_t = kv[0:2].reshape(128, 256)
    val = kv[2:4].reshape(128, 256).astype(F32).T.astype(BF)
    factor = 1.0 / HD**0.5
    c8 = lax.broadcasted_iota(jnp.int32, (8, 512), 1)
    r8 = lax.broadcasted_iota(jnp.int32, (8, 512), 0)
    own_cached = (c8 >> 6) == r8
    pos = c8 & 63
    cn = lax.broadcasted_iota(jnp.int32, (64, 256), 1)
    rn = lax.broadcasted_iota(jnp.int32, (64, 256), 0)
    seen = (cn >> 6) <= (rn >> 4)

    def batch(b, carry):
        r = pl.multiple_of(b * 8, 8)
        q = jnp.concatenate(
            [qs[pl.ds(s * 64 + r, 8), h * 128 : h * 128 + 128] for s in range(4) for h in range(2)], axis=0
        ).astype(BF)
        keys = kc[pl.ds(r, 8), 0].reshape(512, 128)
        vals = vc[pl.ds(r, 8), 0].reshape(512, 128)
        ok = own_cached & (pos < lens[pl.ds(r, 8), :])
        okc = jnp.concatenate([jnp.where(ok, 0.0, -1e30)] * 8, axis=0)
        okn = seen & ((cn & 63) == (rn & 7) + r)
        sc = jnp.where(okc == 0.0, mm_t(q, keys) * factor, -1e30)
        sn = jnp.where(okn, mm(q, key_t) * factor, -1e30)
        top = jnp.maximum(jnp.max(sc, axis=1, keepdims=True), jnp.max(sn, axis=1, keepdims=True))
        ec, en = jnp.exp(sc - top), jnp.exp(sn - top)
        total = jnp.sum(ec, axis=1, keepdims=True) + jnp.sum(en, axis=1, keepdims=True)
        pc, pn = (ec / total).astype(BF), (en / total).astype(BF)
        out = mm(pc, vals) + mm(pn, val)
        for s in range(4):
            for h in range(2):
                n = (s * 2 + h) * 8
                cs[pl.ds(s * 64 + r, 8), h * 128 : h * 128 + 128] = out[n : n + 8]
        return carry

    lax.fori_loop(0, 8, batch, 0)
    ctx[...] = cs[...].astype(BF)


def merge_o_kernel(ids, *refs):
    blocks = refs[:8]
    weights = refs[8:12]
    out, hold = refs[12:]
    x, c, y = ids[0], ids[2], ids[3]
    ks = (x - y + 4) & 3
    for k in range(4):
        for o in range(2):

            @pl.when(ks == k)
            def _():
                hold[o] = blocks[2 * k + o][0:640, :]

    order = [rank_order(ids, h, 64) for h in range(2)]
    for k in range(4):
        at = pl.multiple_of(656 + 16 * ((y - k + 4) & 3), 16)
        stack = jnp.concatenate([b[pl.ds(at, 16), :] for b in blocks], axis=0)
        lower = jnp.concatenate([2.0 * mm(order[h], stack) for h in range(2)], axis=1)
        lower_t = lower.T.astype(BF)
        for zz in range(4):
            zh, cc = zz // 2, zz % 2
            o = c + cc - 2 * c * cc
            u = hold[o, zh * 320 : zh * 320 + 320, :]
            w = weights[k][:, zz * 320 : zz * 320 + 320].astype(F32)
            out[k, zz] = (w + mm_t(lower_t, u)).astype(BF)


def project_kernel(c0, c1, c2, c3, merged, out):
    for zz in range(4):
        total = mm(c0[...], merged[0, zz])
        for k, ref in ((1, c1), (2, c2), (3, c3)):
            total = total + mm(ref[...], merged[k, zz])
        out[zz] = total.astype(BF)


def sum_kernel(parts, out):
    total = parts[0].astype(F32)
    for k in range(1, 4):
        total = total + parts[k].astype(F32)
    out[...] = total.astype(BF).reshape(out.shape)


def shift(axis, size, by):
    return [(i, (i + by) % size) for i in range(size)]


def kv_pairs(k):
    pairs = []
    for s in range(16):
        a, e, b = s // 4, (s % 4) // 2, s % 2
        pairs.append((s, (2 * (a % 2) + e) * 4 + ((a // 2) * 2 + b + k) % 4))
    return pairs


def local(states, wq, wkv, wo, qa_low, qa_up, oa_low, oa_up, kcache, vcache, lens):
    x, zh, c, y, z = (lax.axis_index(a) for a in ("x", "zh", "c", "y", "z"))
    ids = jnp.stack([x, zh, c, y, z]).astype(jnp.int32)

    def halves(a):
        return jnp.concatenate([a[:, :128], a[:, 128:]], axis=0)

    def block(target):
        return lax.dynamic_slice_in_dim(wo, target * 1280, 1280, 1)

    weights = [block(y)]
    for s in (1, 2, 3):
        weights.append(lax.ppermute(block((y + s) % 4), "y", shift("y", 4, s)))

    message = jnp.concatenate(
        [
            jnp.concatenate([qa_low, oa_up], axis=1),
            jnp.zeros((12, 128), BF),
            halves(qa_up),
            halves(oa_low),
        ],
        axis=0,
    )
    got = lax.all_to_all(
        jnp.broadcast_to(message[None], (32, MSG, 128)), ("zh", "y", "z"), 0, 0, tiled=True
    )
    mine = pl.pallas_call(
        sort_kernel,
        out_shape=jax.ShapeDtypeStruct((XROWS, 128), BF),
        in_specs=[SMEM, pl.BlockSpec(memory_space=pltpu.VMEM)],
        compiler_params=params(),
        name="sort_rows",
    )(ids, got)
    blocks = []
    for s in range(4):
        part = mine if s == 0 else lax.ppermute(mine, "x", shift("x", 4, s))
        blocks += [part, lax.ppermute(part, "c", [(0, 1), (1, 0)])]

    normed, kv_t = pl.pallas_call(
        norm_kernel,
        out_shape=(
            jax.ShapeDtypeStruct((8, ROWS, 640), BF),
            jax.ShapeDtypeStruct((64, ROWS), BF),
        ),
        scratch_shapes=[pltpu.VMEM((ROWS, WIDTH), BF)],
        compiler_params=params(),
        cost_estimate=pl.CostEstimate(flops=170_000_000, bytes_accessed=8_000_000, transcendentals=0),
        name="norm_kv",
    )(states.reshape(ROWS, WIDTH), wkv.T)
    new_kv = [lax.ppermute(kv_t, TP, kv_pairs(k)) for k in range(4)]

    vmem = pl.BlockSpec(memory_space=pltpu.VMEM)
    one = pl.BlockSpec((64, 1, 64, 128), lambda i, ids, head: (0, head[0], 0, 0))

    def whole(shape):
        return pl.BlockSpec(shape, lambda i, ids, head: (0,) * len(shape))

    ctx = pl.pallas_call(
        attend_kernel,
        out_shape=jax.ShapeDtypeStruct((ROWS, 256), BF),
        grid_spec=pltpu.PrefetchScalarGridSpec(
            num_scalar_prefetch=2,
            grid=(1,),
            in_specs=[whole((XROWS, 128))] * 8
            + [whole((WIDTH, 256)), whole((8, ROWS, 640)), one, one]
            + [whole((64, 256))] * 4
            + [whole((64, 1))],
            out_specs=whole((ROWS, 256)),
            scratch_shapes=[
                pltpu.VMEM((4, 64, 256), BF),
                pltpu.VMEM((ROWS, 256), F32),
                pltpu.VMEM((ROWS, 256), F32),
            ],
        ),
        compiler_params=params(),
        cost_estimate=pl.CostEstimate(flops=1_000_000_000, bytes_accessed=10_000_000, transcendentals=400_000),
        name="attend",
    )(ids, y.reshape(1).astype(jnp.int32), *blocks, wq, normed, kcache, vcache, *new_kv, lens.reshape(64, 1))

    others = [lax.ppermute(ctx, "y", shift("y", 4, s)) for s in (1, 2, 3)]
    merged = pl.pallas_call(
        merge_o_kernel,
        out_shape=jax.ShapeDtypeStruct((4, 4, 256, 320), BF),
        in_specs=[SMEM] + [vmem] * 12,
        scratch_shapes=[pltpu.VMEM((2, 640, 128), BF)],
        compiler_params=params(),
        cost_estimate=pl.CostEstimate(flops=340_000_000, bytes_accessed=8_000_000, transcendentals=0),
        name="merge_o",
    )(ids, *blocks, *weights)
    parts = pl.pallas_call(
        project_kernel,
        out_shape=jax.ShapeDtypeStruct((4, ROWS, 320), BF),
        compiler_params=params(),
        cost_estimate=pl.CostEstimate(flops=680_000_000, bytes_accessed=4_000_000, transcendentals=0),
        name="project",
    )(ctx, *others, merged)
    parts = lax.all_to_all(parts, "z", 0, 0, tiled=True)
    return pl.pallas_call(
        sum_kernel,
        out_shape=jax.ShapeDtypeStruct((4, 64, 320), BF),
        compiler_params=params(),
        name="sum_parts",
    )(parts)


def solution(mesh):
    fine = Mesh(np.asarray(mesh.devices).reshape(NX, NZH, NC, NY, NZ), GROUP + TP)
    every = GROUP + TP
    in_specs = (
        P(None, GROUP, None),
        P(None, TP),
        P(None, TP),
        P(TP, None),
        P(every, None),
        P(GROUP, TP),
        P(GROUP, TP),
        P(every, None),
        P(GROUP, None, None, None),
        P(GROUP, None, None, None),
        P(GROUP),
    )
    out_specs = P(None, GROUP, TP)
    return jax.shard_map(local, mesh=fine, in_specs=in_specs, out_specs=out_specs, check_vma=False)
```

```python
import jax
import jax.numpy as jnp
import numpy as np
from jax import lax
from jax.experimental import pallas as pl
from jax.experimental.pallas import tpu as pltpu
from jax.sharding import Mesh
from jax.sharding import PartitionSpec as P

HD = 128
STEPS = 4
ROWS = 256
WIDTH = 5120
NX, NZH, NC, NY, NZ = 4, 2, 2, 4, 4
GROUP = ("x", "zh", "c")
TP = ("y", "z")
BF = jnp.bfloat16
F32 = jnp.float32
MSG = 40
XROWS = 720

SMEM = pl.BlockSpec(memory_space=pltpu.SMEM)


def params(mib):
    return pltpu.CompilerParams(vmem_limit_bytes=mib * 1024 * 1024)


def mm(a, b):
    return jnp.dot(a, b, preferred_element_type=F32)


def mm_t(a, b):
    return lax.dot_general(a, b, (((1,), (1,)), ((), ())), preferred_element_type=F32)


def pack_kernel(ids, low, up, q_up, o_low, wo, out, own, *rest):
    sent, (low_v, up_v, qu_v, ol_v, sems) = rest[:3], rest[3:]
    c, y = ids[2], ids[3]
    half = pl.ds(pl.multiple_of(c * 128, 128), 128)
    small = [
        pltpu.make_async_copy(a, b, sems.at[4 + n])
        for n, (a, b) in enumerate(((low, low_v), (up, up_v), (q_up, qu_v), (o_low, ol_v)))
    ]
    large = [pltpu.make_async_copy(wo.at[:, pl.ds(pl.multiple_of(y * 1280, 1280), 1280)], own, sems.at[0])]
    for n, ref in enumerate(sent):
        at = pl.multiple_of(((y + n + 1) & 3) * 1280, 1280)
        large.append(pltpu.make_async_copy(wo.at[half, pl.ds(at, 1280)], ref, sems.at[n + 1]))
    for copy in small + large:
        copy.start()
    for copy in small:
        copy.wait()

    def halves(ref):
        a = ref[...].astype(F32)
        return [a[:, :128], a[:, 128:]]

    first = jnp.concatenate([low_v[...].astype(F32), up_v[...].astype(F32)], axis=1)
    rows = [first, jnp.zeros((4, 128), F32)] + halves(qu_v) + halves(ol_v)
    message = jnp.concatenate(rows, axis=0).astype(BF)

    def write(i, carry):
        out[i] = message
        return carry

    lax.fori_loop(0, out.shape[0], write, 0)
    for copy in large:
        copy.wait()


def norm_kernel(states, wkv_t, blocks, kv_t, x_v, w_v, flat, out_v, sems):
    loads = [pltpu.make_async_copy(states.at[n], x_v.at[n], sems.at[n]) for n in range(STEPS)]
    loads.append(pltpu.make_async_copy(wkv_t, w_v, sems.at[STEPS]))
    for copy in loads:
        copy.start()
    for n in range(STEPS):
        loads[n].wait()

        def rows(i, carry):
            r = pl.multiple_of(i * 32, 32)
            x = x_v[n, pl.ds(r, 32), :].astype(F32)
            scale = lax.rsqrt(jnp.mean(x * x, axis=1, keepdims=True) + 1e-06)
            normed = (x * scale).astype(BF)
            to = pl.ds(pl.multiple_of(n * 64 + r, 32), 32)
            flat[to, :] = normed
            for xc in range(8):
                g = (xc // 2) * 4 + xc % 2
                out_v[xc, to, :] = jnp.concatenate(
                    [normed[:, g * 320 : g * 320 + 320], normed[:, g * 320 + 640 : g * 320 + 960]], axis=1
                )
            return carry

        lax.fori_loop(0, 2, rows, 0)
    store = pltpu.make_async_copy(out_v, blocks, sems.at[0])
    store.start()
    loads[STEPS].wait()
    kv_t[...] = mm_t(flat[...], w_v[...]).T.astype(BF)
    store.wait()


def sort_kernel(ids, got, out):
    i = lax.broadcasted_iota(jnp.int32, (80, MSG), 0)
    j = lax.broadcasted_iota(jnp.int32, (80, MSG), 1)
    picks = [jnp.where((j == i - 20 * p) & (j < 20), 1.0, 0.0).astype(BF) for p in range(4)]
    for q in range(8):
        rows = mm(picks[0], got[4 * q])
        for p in range(1, 4):
            rows = rows + mm(picks[p], got[4 * q + p])
        out[80 * q : 80 * q + 80, :] = rows.astype(BF)
    y, z = ids[3], ids[4]
    own = [got[zh * 16 + y * NZ + z].astype(F32)[24:32] for zh in range(2)]
    out[640:656, :] = jnp.concatenate(own, axis=0).astype(BF)
    for yy in range(NY):
        part = [got[zh * 16 + yy * NZ + z].astype(F32)[32:40] for zh in range(2)]
        out[656 + 16 * yy : 672 + 16 * yy, :] = jnp.concatenate(part, axis=0).astype(BF)


def rank_order(ids, half, first):
    r = lax.broadcasted_iota(jnp.int32, (128, 128), 0)
    j = lax.broadcasted_iota(jnp.int32, (128, 128), 1)
    x, c = ids[0], ids[2]
    k, o = (j >> 5) & 3, (j >> 4) & 1
    zh, h, i = (j >> 3) & 1, (j >> 2) & 1, j & 3
    xs = (x - k + 4) & 3
    rank = (xs * 4 + zh * 2 + (c + o - 2 * c * o)) * 4 + i
    return jnp.where((h == half) & (r == rank + first), 1.0, 0.0).astype(BF)


def attend_kernel(ids, *refs):
    blocks = refs[:8]
    wq_h, normed_h, kc_h, vc_h, kv0, kv1, kv2, kv3, lens, ctx = refs[8:18]
    kv, qs, cs, wq, normed, kc, vc, sems = refs[18:]
    x, c, y, z = ids[0], ids[2], ids[3], ids[4]
    steps, loads = [], []
    for n in range(8):
        k, o = n // 2, n % 2
        at = ((x - k + 4) & 3) * 2 + c + o - 2 * c * o
        row = (at >> 1) * 1280 + (at & 1) * 320
        parts = [pl.ds(pl.multiple_of(row + 640 * zh, 320), 320) for zh in range(2)]
        copies = [
            pltpu.make_async_copy(wq_h.at[parts[0]], wq.at[n, 0:320], sems.at[n, 0]),
            pltpu.make_async_copy(wq_h.at[parts[1]], wq.at[n, 320:640], sems.at[n, 1]),
            pltpu.make_async_copy(normed_h.at[at], normed.at[n], sems.at[n, 2]),
        ]
        steps.append(copies)
    loads = [
        pltpu.make_async_copy(kc_h.at[:, y], kc, sems.at[8, 0]),
        pltpu.make_async_copy(vc_h.at[:, y], vc, sems.at[8, 1]),
    ]
    for copies in steps + [loads]:
        for copy in copies:
            copy.start()
    stack = jnp.concatenate([b[640:656, :] for b in blocks], axis=0)
    upper = jnp.concatenate(
        [2.0 * mm(rank_order(ids, h, 0), stack) for h in range(2)], axis=1
    ).astype(BF)
    total = jnp.zeros((ROWS, 256), F32)
    for n in range(8):
        rank = mm(blocks[n][0:640, :], upper)
        for copy in steps[n]:
            copy.wait()
        merged = (wq[n].astype(F32) + rank).astype(BF)
        total = total + mm(normed[n], merged)
    qs[...] = total.astype(BF).astype(F32)
    for k, ref in enumerate((kv0, kv1, kv2, kv3)):
        kv[(z - k + 4) & 3] = ref[...]
    key_t = kv[0:2].reshape(128, 256)
    val = kv[2:4].reshape(128, 256).astype(F32).T.astype(BF)
    for copy in loads:
        copy.wait()
    factor = 1.0 / HD**0.5
    c8 = lax.broadcasted_iota(jnp.int32, (8, 512), 1)
    r8 = lax.broadcasted_iota(jnp.int32, (8, 512), 0)
    own_cached = (c8 >> 6) == r8
    pos = c8 & 63
    cn = lax.broadcasted_iota(jnp.int32, (64, 256), 1)
    rn = lax.broadcasted_iota(jnp.int32, (64, 256), 0)
    seen = (cn >> 6) <= (rn >> 4)

    def batch(b, carry):
        r = pl.multiple_of(b * 8, 8)
        q = jnp.concatenate(
            [qs[pl.ds(s * 64 + r, 8), h * 128 : h * 128 + 128] for s in range(4) for h in range(2)], axis=0
        ).astype(BF)
        keys = kc[pl.ds(r, 8)].reshape(512, 128)
        vals = vc[pl.ds(r, 8)].reshape(512, 128)
        length = jnp.zeros((8, 512), jnp.int32)
        for i in range(8):
            length = jnp.where(r8 == i, lens[r + i], length)
        ok = jnp.where(own_cached & (pos < length), 1.0, 0.0)
        okc = jnp.concatenate([ok] * 8, axis=0) > 0.5
        okn = seen & ((cn & 63) == (rn & 7) + r)
        sc = jnp.where(okc, mm_t(q, keys) * factor, -1e30)
        sn = jnp.where(okn, mm(q, key_t) * factor, -1e30)
        top = jnp.maximum(jnp.max(sc, axis=1, keepdims=True), jnp.max(sn, axis=1, keepdims=True))
        ec, en = jnp.exp(sc - top), jnp.exp(sn - top)
        total = jnp.sum(ec, axis=1, keepdims=True) + jnp.sum(en, axis=1, keepdims=True)
        pc, pn = (ec / total).astype(BF), (en / total).astype(BF)
        out = mm(pc, vals) + mm(pn, val)
        for s in range(4):
            for h in range(2):
                n = (s * 2 + h) * 8
                cs[pl.ds(s * 64 + r, 8), h * 128 : h * 128 + 128] = out[n : n + 8]
        return carry

    lax.fori_loop(0, 8, batch, 0, unroll=2)
    ctx[...] = cs[...].astype(BF)


def merge_o_kernel(ids, *refs):
    blocks = refs[:8]
    own = refs[8]
    same, other = refs[9:12], refs[12:15]
    out, hold, low = refs[15:]
    x, c, y = ids[0], ids[2], ids[3]
    ks = (x - y + 4) & 3
    for k in range(4):
        for o in range(2):

            @pl.when(ks == k)
            def _():
                hold[o] = blocks[2 * k + o][0:640, :]

    order = [rank_order(ids, h, 64) for h in range(2)]
    for k in range(4):
        yy = (y - k + 4) & 3
        at = pl.multiple_of(656 + 16 * yy, 16)
        stack = jnp.concatenate([b[pl.ds(at, 16), :] for b in blocks], axis=0)
        lower = jnp.concatenate([2.0 * mm(order[h], stack) for h in range(2)], axis=1)
        low[...] = lower.T.astype(BF)
        for zz in range(4):
            zh, cc = zz // 2, zz % 2
            o = c + cc - 2 * c * cc
            u = hold[o, zh * 320 : zh * 320 + 320, :]
            cols = slice(zz * 320, zz * 320 + 320)
            if k == 0:
                out[k, zz] = (own[:, cols].astype(F32) + mm_t(low[...], u)).astype(BF)
            else:
                for ref, core in ((same[k - 1], c), (other[k - 1], 1 - c)):
                    at = pl.ds(pl.multiple_of(core * 128, 128), 128)
                    out[k, zz, at] = (ref[:, cols].astype(F32) + mm_t(low[at, :], u)).astype(BF)


def project_kernel(c0, c1, c2, c3, merged, out):
    for zz in range(4):
        total = mm(c0[...], merged[0, zz])
        for k, ref in ((1, c1), (2, c2), (3, c3)):
            total = total + mm(ref[...], merged[k, zz])
        total = total.astype(BF)
        out[zz, 0:256] = total[:, 0:128]
        out[zz, 256:512] = total[:, 128:256]
        out[zz, 512:640] = jnp.concatenate([total[0:128, 256:320], total[128:256, 256:320]], axis=1)


def sum_kernel(parts, out):
    total = parts[0].astype(F32)
    for k in range(1, 4):
        total = total + parts[k].astype(F32)
    tail = jnp.concatenate([total[512:640, :64], total[512:640, 64:]], axis=0)
    full = jnp.concatenate([total[0:256], total[256:512], tail], axis=1).astype(BF)
    out[...] = full.reshape(out.shape)


def far(a):
    return pltpu.with_memory_space_constraint(a, pltpu.HBM)


def shift(axis, size, by):
    return [(i, (i + by) % size) for i in range(size)]


def kv_pairs(k):
    pairs = []
    for s in range(16):
        a, e, b = s // 4, (s % 4) // 2, s % 2
        pairs.append((s, (2 * (a % 2) + e) * 4 + ((a // 2) * 2 + b + k) % 4))
    return pairs


def local(states, wq, wkv, wo, qa_low, qa_up, oa_low, oa_up, kcache, vcache, lens):
    x, zh, c, y, z = (lax.axis_index(a) for a in ("x", "zh", "c", "y", "z"))
    ids = jnp.stack([x, zh, c, y, z]).astype(jnp.int32)

    vmem = pl.BlockSpec(memory_space=pltpu.VMEM)
    hbm = pl.BlockSpec(memory_space=pltpu.HBM)

    def array(*shape):
        return jax.ShapeDtypeStruct(shape, BF)

    messages, w_own, *w_sent = pl.pallas_call(
        pack_kernel,
        out_shape=(array(32, MSG, 128), array(256, 1280)) + (array(128, 1280),) * 3,
        in_specs=[SMEM] + [hbm] * 5,
        scratch_shapes=[
            pltpu.VMEM((20, 64), BF),
            pltpu.VMEM((20, 64), BF),
            pltpu.VMEM((4, 256), BF),
            pltpu.VMEM((4, 256), BF),
            pltpu.SemaphoreType.DMA((8,)),
        ],
        compiler_params=params(8),
        name="pack",
    )(ids, *(far(a) for a in (qa_low, oa_up, qa_up, oa_low, wo)))
    got = lax.all_to_all(messages, ("zh", "y", "z"), 0, 0, tiled=True)

    normed, kv_t = pl.pallas_call(
        norm_kernel,
        out_shape=(pltpu.HBM((8, ROWS, 640), BF), array(64, ROWS)),
        in_specs=[hbm, hbm],
        out_specs=(hbm, vmem),
        scratch_shapes=[
            pltpu.VMEM((STEPS, 64, WIDTH), BF),
            pltpu.VMEM((64, WIDTH), BF),
            pltpu.VMEM((ROWS, WIDTH), BF),
            pltpu.VMEM((8, ROWS, 640), BF),
            pltpu.SemaphoreType.DMA((5,)),
        ],
        compiler_params=params(24),
        cost_estimate=pl.CostEstimate(flops=170_000_000, bytes_accessed=8_000_000, transcendentals=0),
        name="norm_kv",
    )(far(states), far(wkv.T))
    new_kv = [lax.ppermute(kv_t, TP, kv_pairs(k)) for k in range(4)]

    swap = [(0, 1), (1, 0)]
    w_same = [lax.ppermute(w_sent[0], "y", shift("y", 4, 1))]
    got, normed, w_same[0] = lax.optimization_barrier((got, normed, w_same[0]))
    mine = pl.pallas_call(
        sort_kernel,
        out_shape=array(XROWS, 128),
        in_specs=[SMEM, vmem],
        compiler_params=params(6),
        name="sort_rows",
    )(ids, got)
    mine, w_second, *new_kv = lax.optimization_barrier((mine, w_sent[1], *new_kv))
    w_same.append(lax.ppermute(w_second, "y", shift("y", 4, 2)))
    parts = [mine] + [lax.ppermute(mine, "x", shift("x", 4, s)) for s in (1, 2, 3)]
    *parts, w_same[1], w_third = lax.optimization_barrier((*parts, w_same[1], w_sent[2]))
    w_same.append(lax.ppermute(w_third, "y", shift("y", 4, 3)))
    blocks = []
    for part in parts:
        blocks += [part, lax.ppermute(part, "c", swap)]

    ctx = pl.pallas_call(
        attend_kernel,
        out_shape=array(ROWS, 256),
        in_specs=[SMEM] + [vmem] * 8 + [hbm] * 4 + [vmem] * 4 + [SMEM],
        scratch_shapes=[
            pltpu.VMEM((4, 64, 256), BF),
            pltpu.VMEM((ROWS, 256), F32),
            pltpu.VMEM((ROWS, 256), F32),
            pltpu.VMEM((8, 640, 256), BF),
            pltpu.VMEM((8, ROWS, 640), BF),
            pltpu.VMEM((64, 64, 128), BF),
            pltpu.VMEM((64, 64, 128), BF),
            pltpu.SemaphoreType.DMA((9, 3)),
        ],
        compiler_params=params(24),
        cost_estimate=pl.CostEstimate(flops=1_000_000_000, bytes_accessed=10_000_000, transcendentals=400_000),
        name="attend",
    )(ids, *blocks, far(wq), far(normed), far(kcache), far(vcache), *new_kv, lens)

    others = [lax.ppermute(ctx, "y", shift("y", 4, s)) for s in (1, 2, 3)]
    w_other = [lax.ppermute(w, "c", swap) for w in w_same]
    merged = pl.pallas_call(
        merge_o_kernel,
        out_shape=array(4, 4, 256, 320),
        in_specs=[SMEM] + [vmem] * 15,
        scratch_shapes=[pltpu.VMEM((2, 640, 128), BF), pltpu.VMEM((256, 128), BF)],
        compiler_params=params(20),
        cost_estimate=pl.CostEstimate(flops=340_000_000, bytes_accessed=8_000_000, transcendentals=0),
        name="merge_o",
    )(ids, *blocks, w_own, *w_same, *w_other)
    parts = pl.pallas_call(
        project_kernel,
        out_shape=array(4, 640, 128),
        compiler_params=params(16),
        cost_estimate=pl.CostEstimate(flops=680_000_000, bytes_accessed=4_000_000, transcendentals=0),
        name="project",
    )(ctx, *others, merged)
    parts = lax.all_to_all(parts, "z", 0, 0, tiled=True)
    return pl.pallas_call(
        sum_kernel,
        out_shape=array(4, 64, 320),
        compiler_params=params(6),
        name="sum_parts",
    )(parts)


def solution(mesh):
    fine = Mesh(np.asarray(mesh.devices).reshape(NX, NZH, NC, NY, NZ), GROUP + TP)
    every = GROUP + TP
    in_specs = (
        P(None, GROUP, None),
        P(None, TP),
        P(None, TP),
        P(TP, None),
        P(every, None),
        P(GROUP, TP),
        P(GROUP, TP),
        P(every, None),
        P(GROUP, None, None, None),
        P(GROUP, None, None, None),
        P(GROUP),
    )
    out_specs = P(None, GROUP, TP)
    return jax.shard_map(local, mesh=fine, in_specs=in_specs, out_specs=out_specs, check_vma=False)
```

```python
import jax
import jax.numpy as jnp
import numpy as np
from jax import lax
from jax.experimental import pallas as pl
from jax.experimental.pallas import tpu as pltpu
from jax.sharding import Mesh
from jax.sharding import PartitionSpec as P

HD = 128
STEPS = 4
ROWS = 256
WIDTH = 5120
NX, NZH, NC, NY, NZ = 4, 2, 2, 4, 4
GROUP = ("x", "zh", "c")
TP = ("y", "z")
BF = jnp.bfloat16
F32 = jnp.float32
MSG = 40
XROWS = 720

SMEM = pl.BlockSpec(memory_space=pltpu.SMEM)


def params(mib):
    return pltpu.CompilerParams(vmem_limit_bytes=mib * 1024 * 1024)


def mm(a, b):
    return jnp.dot(a, b, preferred_element_type=F32)


def mm_t(a, b):
    return lax.dot_general(a, b, (((1,), (1,)), ((), ())), preferred_element_type=F32)


def pack_kernel(low, up, q_up, o_low, out, low_v, up_v, qu_v, ol_v, sems):
    copies = [
        pltpu.make_async_copy(a, b, sems.at[n])
        for n, (a, b) in enumerate(((low, low_v), (up, up_v), (q_up, qu_v), (o_low, ol_v)))
    ]
    for copy in copies:
        copy.start()
    for copy in copies:
        copy.wait()

    def halves(ref):
        a = ref[...].astype(F32)
        return [a[:, :128], a[:, 128:]]

    first = jnp.concatenate([low_v[...].astype(F32), up_v[...].astype(F32)], axis=1)
    rows = [first, jnp.zeros((4, 128), F32)] + halves(qu_v) + halves(ol_v)
    message = jnp.concatenate(rows, axis=0).astype(BF)

    def write(i, carry):
        out[i] = message
        return carry

    lax.fori_loop(0, out.shape[0], write, 0)


def norm_kernel(ids, states, wkv_t, wo, blocks, kv_t, w1, w2, w3, x_v, w_v, flat, out_v, cut, sems):
    c, y = ids[2], ids[3]
    half = pl.ds(pl.multiple_of(c * 128, 128), 128)
    loads = [pltpu.make_async_copy(states.at[n], x_v.at[n], sems.at[n]) for n in range(STEPS)]
    loads.append(pltpu.make_async_copy(wkv_t, w_v, sems.at[STEPS]))
    cuts, puts = [], []
    for n, ref in enumerate((w1, w2, w3)):
        at = pl.multiple_of(((y + n + 1) & 3) * 1280, 1280)
        cuts.append(pltpu.make_async_copy(wo.at[half, pl.ds(at, 1280)], cut.at[n], sems.at[5 + n]))
        puts.append(pltpu.make_async_copy(cut.at[n], ref, sems.at[8 + n]))
    for copy in loads + cuts:
        copy.start()
    for n in range(STEPS):
        loads[n].wait()

        def rows(i, carry):
            r = pl.multiple_of(i * 32, 32)
            x = x_v[n, pl.ds(r, 32), :].astype(F32)
            scale = lax.rsqrt(jnp.mean(x * x, axis=1, keepdims=True) + 1e-06)
            normed = (x * scale).astype(BF)
            to = pl.ds(pl.multiple_of(n * 64 + r, 32), 32)
            flat[to, :] = normed
            for xc in range(8):
                g = (xc // 2) * 4 + xc % 2
                out_v[xc, to, :] = jnp.concatenate(
                    [normed[:, g * 320 : g * 320 + 320], normed[:, g * 320 + 640 : g * 320 + 960]], axis=1
                )
            return carry

        lax.fori_loop(0, 2, rows, 0)
    for cut_copy, put in zip(cuts, puts):
        cut_copy.wait()
        put.start()
    store = pltpu.make_async_copy(out_v, blocks, sems.at[11])
    store.start()
    loads[STEPS].wait()
    kv_t[...] = mm_t(flat[...], w_v[...]).T.astype(BF)
    for copy in puts + [store]:
        copy.wait()


def sort_kernel(ids, got, out):
    i = lax.broadcasted_iota(jnp.int32, (80, MSG), 0)
    j = lax.broadcasted_iota(jnp.int32, (80, MSG), 1)
    picks = [jnp.where((j == i - 20 * p) & (j < 20), 1.0, 0.0).astype(BF) for p in range(4)]
    for q in range(8):
        rows = mm(picks[0], got[4 * q])
        for p in range(1, 4):
            rows = rows + mm(picks[p], got[4 * q + p])
        out[80 * q : 80 * q + 80, :] = rows.astype(BF)
    y, z = ids[3], ids[4]
    own = [got[zh * 16 + y * NZ + z].astype(F32)[24:32] for zh in range(2)]
    out[640:656, :] = jnp.concatenate(own, axis=0).astype(BF)
    for yy in range(NY):
        part = [got[zh * 16 + yy * NZ + z].astype(F32)[32:40] for zh in range(2)]
        out[656 + 16 * yy : 672 + 16 * yy, :] = jnp.concatenate(part, axis=0).astype(BF)


def rank_order(ids, half, first):
    r = lax.broadcasted_iota(jnp.int32, (128, 128), 0)
    j = lax.broadcasted_iota(jnp.int32, (128, 128), 1)
    x, c = ids[0], ids[2]
    k, o = (j >> 5) & 3, (j >> 4) & 1
    zh, h, i = (j >> 3) & 1, (j >> 2) & 1, j & 3
    xs = x ^ k
    rank = (xs * 4 + zh * 2 + (c + o - 2 * c * o)) * 4 + i
    return jnp.where((h == half) & (r == rank + first), 1.0, 0.0).astype(BF)


def attend_kernel(ids, *refs):
    blocks = refs[:8]
    wq, normed_h, kc_h, vc_h = refs[8:12]
    pieces, lens, ctx = refs[12:16], refs[16], refs[17]
    kv, qs, cs, normed, kc, vc, sems = refs[18:]
    x, c, y, z = ids[0], ids[2], ids[3], ids[4]
    loads = [
        pltpu.make_async_copy(kc_h.at[:, y], kc, sems.at[0]),
        pltpu.make_async_copy(vc_h.at[:, y], vc, sems.at[1]),
    ]
    ats = [(x ^ (n // 2)) * 2 + c + n % 2 - 2 * c * (n % 2) for n in range(8)]
    steps = [pltpu.make_async_copy(normed_h.at[at], normed.at[n], sems.at[2 + n]) for n, at in enumerate(ats)]
    for copy in steps + loads:
        copy.start()
    stack = jnp.concatenate([b[640:656, :] for b in blocks], axis=0)
    upper = jnp.concatenate(
        [2.0 * mm(rank_order(ids, h, 0), stack) for h in range(2)], axis=1
    ).astype(BF)
    total = jnp.zeros((ROWS, 256), F32)
    for n in range(8):
        rank = mm(blocks[n][0:640, :], upper)
        at = ats[n]
        row = pl.multiple_of((at >> 1) * 1280 + (at & 1) * 320, 320)
        base = jnp.concatenate([wq[pl.ds(row, 320), :], wq[pl.ds(row + 640, 320), :]], axis=0)
        merged = (base.astype(F32) + rank).astype(BF)
        steps[n].wait()
        total = total + mm(normed[n], merged)
    qs[...] = total.astype(BF).astype(F32)
    for k, ref in enumerate(pieces):
        kv[(z ^ k) & 3] = ref[...]
    key_t = kv[0:2].reshape(128, 256)
    val = kv[2:4].reshape(128, 256).astype(F32).T.astype(BF)
    for copy in loads:
        copy.wait()
    factor = 1.0 / HD**0.5
    c8 = lax.broadcasted_iota(jnp.int32, (8, 512), 1)
    r8 = lax.broadcasted_iota(jnp.int32, (8, 512), 0)
    own_cached = (c8 >> 6) == r8
    pos = c8 & 63
    cn = lax.broadcasted_iota(jnp.int32, (64, 256), 1)
    rn = lax.broadcasted_iota(jnp.int32, (64, 256), 0)
    seen = (cn >> 6) <= (rn >> 4)

    def batch(b, carry):
        r = pl.multiple_of(b * 8, 8)
        q = jnp.concatenate(
            [qs[pl.ds(s * 64 + r, 8), h * 128 : h * 128 + 128] for s in range(4) for h in range(2)], axis=0
        ).astype(BF)
        keys = kc[pl.ds(r, 8)].reshape(512, 128)
        vals = vc[pl.ds(r, 8)].reshape(512, 128)
        length = jnp.zeros((8, 512), jnp.int32)
        for i in range(8):
            length = jnp.where(r8 == i, lens[r + i], length)
        ok = jnp.where(own_cached & (pos < length), 1.0, 0.0)
        okc = jnp.concatenate([ok] * 8, axis=0) > 0.5
        okn = seen & ((cn & 63) == (rn & 7) + r)
        sc = jnp.where(okc, mm_t(q, keys) * factor, -1e30)
        sn = jnp.where(okn, mm(q, key_t) * factor, -1e30)
        top = jnp.maximum(jnp.max(sc, axis=1, keepdims=True), jnp.max(sn, axis=1, keepdims=True))
        ec, en = jnp.exp(sc - top), jnp.exp(sn - top)
        total = jnp.sum(ec, axis=1, keepdims=True) + jnp.sum(en, axis=1, keepdims=True)
        inverse = 1.0 / total
        pc, pn = (ec * inverse).astype(BF), (en * inverse).astype(BF)
        out = mm(pc, vals) + mm(pn, val)
        for s in range(4):
            for h in range(2):
                n = (s * 2 + h) * 8
                cs[pl.ds(s * 64 + r, 8), h * 128 : h * 128 + 128] = out[n : n + 8]
        return carry

    lax.fori_loop(0, 8, batch, 0, unroll=4)
    ctx[...] = cs[...].astype(BF)


def merge_o_kernel(ids, *refs):
    blocks = refs[:8]
    wo = refs[8]
    same, other = refs[9:12], refs[12:15]
    out, hold, low, own, sem = refs[15:]
    x, c, y = ids[0], ids[2], ids[3]
    load = pltpu.make_async_copy(wo.at[:, pl.ds(pl.multiple_of(y * 1280, 1280), 1280)], own, sem)
    load.start()
    ks = x ^ y
    for k in range(4):
        for o in range(2):

            @pl.when(ks == k)
            def _():
                hold[o] = blocks[2 * k + o][0:640, :]

    order = [rank_order(ids, h, 64) for h in range(2)]
    for k in (1, 2, 3, 0):
        if k == 0:
            load.wait()
        yy = (y - k + 4) & 3
        at = pl.multiple_of(656 + 16 * yy, 16)
        stack = jnp.concatenate([b[pl.ds(at, 16), :] for b in blocks], axis=0)
        lower = jnp.concatenate([2.0 * mm(order[h], stack) for h in range(2)], axis=1)
        low[...] = lower.T.astype(BF)
        for zz in range(4):
            zh, cc = zz // 2, zz % 2
            o = c + cc - 2 * c * cc
            u = hold[o, zh * 320 : zh * 320 + 320, :]
            cols = slice(zz * 320, zz * 320 + 320)
            if k == 0:
                out[k, zz] = (own[:, cols].astype(F32) + mm_t(low[...], u)).astype(BF)
            else:
                for ref, core in ((same[k - 1], c), (other[k - 1], 1 - c)):
                    at = pl.ds(pl.multiple_of(core * 128, 128), 128)
                    out[k, zz, at] = (ref[:, cols].astype(F32) + mm_t(low[at, :], u)).astype(BF)


def project_kernel(ids, c0, c1, c2, c3, merged, *out):
    for n in (3, 2, 1, 0):
        zz = ids[4] ^ n
        total = mm(c0[...], merged[0, zz])
        for k, ref in ((1, c1), (2, c2), (3, c3)):
            total = total + mm(ref[...], merged[k, zz])
        total = total.astype(BF)
        out[n][0:256] = total[:, 0:128]
        out[n][256:512] = total[:, 128:256]
        out[n][512:640] = jnp.concatenate([total[0:128, 256:320], total[128:256, 256:320]], axis=1)


def sum_kernel(p0, p1, p2, p3, out):
    total = p0[...].astype(F32) + p1[...].astype(F32) + p2[...].astype(F32) + p3[...].astype(F32)
    tail = jnp.concatenate([total[512:640, :64], total[512:640, 64:]], axis=0)
    full = jnp.concatenate([total[0:256], total[256:512], tail], axis=1).astype(BF)
    out[...] = full.reshape(out.shape)


def near(a):
    return pltpu.with_memory_space_constraint(a, pltpu.VMEM)


def far(a):
    return pltpu.with_memory_space_constraint(a, pltpu.HBM)


def ring(s):
    return [(i, (i + s) % 4) for i in range(4)]


def partner(s):
    return [(i, i ^ s) for i in range(4)]


def kv_pairs(k):
    pairs = []
    for s in range(16):
        a, e, b = s // 4, (s % 4) // 2, s % 2
        pairs.append((s, (2 * (a % 2) + e) * 4 + (((a // 2) * 2 + b) ^ k)))
    return pairs


def local(states, wq, wkv, wo, qa_low, qa_up, oa_low, oa_up, kcache, vcache, lens):
    x, zh, c, y, z = (lax.axis_index(a) for a in ("x", "zh", "c", "y", "z"))
    ids = jnp.stack([x, zh, c, y, z]).astype(jnp.int32)

    vmem = pl.BlockSpec(memory_space=pltpu.VMEM)
    hbm = pl.BlockSpec(memory_space=pltpu.HBM)

    def array(*shape):
        return jax.ShapeDtypeStruct(shape, BF)

    messages = pl.pallas_call(
        pack_kernel,
        out_shape=array(32, MSG, 128),
        in_specs=[hbm] * 4,
        scratch_shapes=[
            pltpu.VMEM((20, 64), BF),
            pltpu.VMEM((20, 64), BF),
            pltpu.VMEM((4, 256), BF),
            pltpu.VMEM((4, 256), BF),
            pltpu.SemaphoreType.DMA((4,)),
        ],
        compiler_params=params(4),
        name="pack",
    )(*(far(a) for a in (qa_low, oa_up, qa_up, oa_low)))
    got = lax.all_to_all(messages, ("zh", "y", "z"), 0, 0, tiled=True)

    normed, kv_t, *w_sent = pl.pallas_call(
        norm_kernel,
        out_shape=(pltpu.HBM((8, ROWS, 640), BF), array(64, ROWS)) + (pltpu.HBM((128, 1280), BF),) * 3,
        in_specs=[SMEM, hbm, hbm, hbm],
        out_specs=(hbm, vmem, hbm, hbm, hbm),
        scratch_shapes=[
            pltpu.VMEM((STEPS, 64, WIDTH), BF),
            pltpu.VMEM((64, WIDTH), BF),
            pltpu.VMEM((ROWS, WIDTH), BF),
            pltpu.VMEM((8, ROWS, 640), BF),
            pltpu.VMEM((3, 128, 1280), BF),
            pltpu.SemaphoreType.DMA((12,)),
        ],
        compiler_params=params(20),
        cost_estimate=pl.CostEstimate(flops=170_000_000, bytes_accessed=8_000_000, transcendentals=0),
        name="norm_kv",
    )(ids, far(states), far(wkv.T), far(wo))
    new_kv = [lax.ppermute(kv_t, TP, kv_pairs(k)) for k in range(4)]

    swap = [(0, 1), (1, 0)]
    got, normed, kv_t = lax.optimization_barrier((got, normed, kv_t))
    mine = pl.pallas_call(
        sort_kernel,
        out_shape=array(XROWS, 128),
        in_specs=[SMEM, vmem],
        compiler_params=params(6),
        name="sort_rows",
    )(ids, got)
    mine, w_sent, new_kv = lax.optimization_barrier((mine, w_sent, new_kv))
    w_first = lax.ppermute(w_sent[0], "y", ring(1))
    w_third = lax.ppermute(w_sent[2], "y", ring(3))
    parts = [mine] + [lax.ppermute(mine, "x", partner(s)) for s in (1, 2, 3)]
    w_first, w_third, w_second = lax.optimization_barrier((w_first, w_third, w_sent[1]))
    w_same = [w_first, lax.ppermute(w_second, "y", ring(2)), w_third]
    blocks = []
    for part in parts:
        blocks += [part, lax.ppermute(part, "c", swap)]

    ctx = pl.pallas_call(
        attend_kernel,
        out_shape=array(ROWS, 256),
        in_specs=[SMEM] + [vmem] * 9 + [hbm] * 3 + [vmem] * 4 + [SMEM],
        scratch_shapes=[
            pltpu.VMEM((4, 64, 256), BF),
            pltpu.VMEM((ROWS, 256), F32),
            pltpu.VMEM((ROWS, 256), F32),
            pltpu.VMEM((8, ROWS, 640), BF),
            pltpu.VMEM((64, 64, 128), BF),
            pltpu.VMEM((64, 64, 128), BF),
            pltpu.SemaphoreType.DMA((10,)),
        ],
        compiler_params=params(24),
        cost_estimate=pl.CostEstimate(flops=1_000_000_000, bytes_accessed=10_000_000, transcendentals=400_000),
        name="attend",
    )(ids, *blocks, near(wq), far(normed), far(kcache), far(vcache), *new_kv, lens)

    others = {s: lax.ppermute(ctx, "y", ring(s)) for s in (1, 3, 2)}
    _, w_same = lax.optimization_barrier((ctx, w_same))
    w_other = [lax.ppermute(w, "c", swap) for w in w_same]
    merged = pl.pallas_call(
        merge_o_kernel,
        out_shape=array(4, 4, 256, 320),
        in_specs=[SMEM] + [vmem] * 8 + [hbm] + [vmem] * 6,
        scratch_shapes=[
            pltpu.VMEM((2, 640, 128), BF),
            pltpu.VMEM((256, 128), BF),
            pltpu.VMEM((256, 1280), BF),
            pltpu.SemaphoreType.DMA(()),
        ],
        compiler_params=params(20),
        cost_estimate=pl.CostEstimate(flops=340_000_000, bytes_accessed=8_000_000, transcendentals=0),
        name="merge_o",
    )(ids, *blocks, far(wo), *w_same, *w_other)
    sums = pl.pallas_call(
        project_kernel,
        out_shape=(array(640, 128),) * 4,
        in_specs=[SMEM] + [vmem] * 5,
        compiler_params=params(16),
        cost_estimate=pl.CostEstimate(flops=680_000_000, bytes_accessed=4_000_000, transcendentals=0),
        name="project",
    )(ids, ctx, others[1], others[2], others[3], merged)
    came = [lax.ppermute(sums[n], "z", partner(n)) for n in (3, 2, 1)]
    return pl.pallas_call(
        sum_kernel,
        out_shape=array(4, 64, 320),
        compiler_params=params(6),
        name="sum_parts",
    )(sums[0], *came)


def solution(mesh):
    fine = Mesh(np.asarray(mesh.devices).reshape(NX, NZH, NC, NY, NZ), GROUP + TP)
    every = GROUP + TP
    in_specs = (
        P(None, GROUP, None),
        P(None, TP),
        P(None, TP),
        P(TP, None),
        P(every, None),
        P(GROUP, TP),
        P(GROUP, TP),
        P(every, None),
        P(GROUP, None, None, None),
        P(GROUP, None, None, None),
        P(GROUP),
    )
    out_specs = P(None, GROUP, TP)
    return jax.shard_map(local, mesh=fine, in_specs=in_specs, out_specs=out_specs, check_vma=False)
```

```python
import jax
import jax.numpy as jnp
import numpy as np
from jax import lax
from jax.experimental import pallas as pl
from jax.experimental.pallas import tpu as pltpu
from jax.sharding import Mesh
from jax.sharding import PartitionSpec as P

HD = 128
STEPS = 4
ROWS = 256
WIDTH = 5120
NX, NZH, NC, NY, NZ = 4, 2, 2, 4, 4
GROUP = ("x", "zh", "c")
TP = ("y", "z")
BF = jnp.bfloat16
F32 = jnp.float32
MSG = 40
XROWS = 720

SMEM = pl.BlockSpec(memory_space=pltpu.SMEM)


def params(mib):
    return pltpu.CompilerParams(vmem_limit_bytes=mib * 1024 * 1024)


def mm(a, b):
    return jnp.dot(a, b, preferred_element_type=F32)


def mm_t(a, b):
    return lax.dot_general(a, b, (((1,), (1,)), ((), ())), preferred_element_type=F32)


def pack_kernel(low, up, q_up, o_low, out, low_v, up_v, qu_v, ol_v, sems):
    copies = [
        pltpu.make_async_copy(a, b, sems.at[n])
        for n, (a, b) in enumerate(((low, low_v), (up, up_v), (q_up, qu_v), (o_low, ol_v)))
    ]
    for copy in copies:
        copy.start()
    for copy in copies:
        copy.wait()

    def halves(ref):
        a = ref[...].astype(F32)
        return [a[:, :128], a[:, 128:]]

    first = jnp.concatenate([low_v[...].astype(F32), up_v[...].astype(F32)], axis=1)
    rows = [first, jnp.zeros((4, 128), F32)] + halves(qu_v) + halves(ol_v)
    message = jnp.concatenate(rows, axis=0).astype(BF)

    def write(i, carry):
        out[i] = message
        return carry

    lax.fori_loop(0, out.shape[0], write, 0)


def norm_kernel(ids, states, wkv_t, wo, normed_h, kv_t, w1, w2, w3, x_v, w_v, flat, cut, sems):
    c, y = ids[2], ids[3]
    half = pl.ds(pl.multiple_of(c * 128, 128), 128)
    loads = [pltpu.make_async_copy(states.at[n], x_v.at[n], sems.at[n]) for n in range(STEPS)]
    loads.append(pltpu.make_async_copy(wkv_t, w_v, sems.at[STEPS]))
    cuts, puts, stores = [], [], []
    for n, ref in enumerate((w1, w2, w3)):
        at = pl.multiple_of(((y + n + 1) & 3) * 1280, 1280)
        cuts.append(pltpu.make_async_copy(wo.at[half, pl.ds(at, 1280)], cut.at[n], sems.at[5 + n]))
        puts.append(pltpu.make_async_copy(cut.at[n], ref, sems.at[8 + n]))
    for copy in loads + cuts:
        copy.start()
    for n in range(STEPS):
        loads[n].wait()

        def rows(i, carry):
            r = pl.multiple_of(i * 32, 32)
            x = x_v[n, pl.ds(r, 32), :].astype(F32)
            scale = lax.rsqrt(jnp.mean(x * x, axis=1, keepdims=True) + 1e-06)
            normed = (x * scale).astype(BF)
            to = pl.ds(pl.multiple_of(n * 64 + r, 32), 32)
            for k in range(10):
                flat[k, to, :] = normed[:, k * 512 : k * 512 + 512]
            return carry

        lax.fori_loop(0, 2, rows, 0, unroll=True)
        span = pl.ds(n * 64, 64)
        stores.append(pltpu.make_async_copy(flat.at[:, span], normed_h.at[:, span], sems.at[11 + n]))
        stores[n].start()
    for cut_copy, put in zip(cuts, puts):
        cut_copy.wait()
        put.start()
    loads[STEPS].wait()
    total = mm_t(flat[0], w_v[:, 0:512])
    for k in range(1, 10):
        total = total + mm_t(flat[k], w_v[:, k * 512 : k * 512 + 512])
    kv_t[...] = total.T.astype(BF)
    for copy in puts + stores:
        copy.wait()


def sort_kernel(ids, got, out):
    i = lax.broadcasted_iota(jnp.int32, (80, MSG), 0)
    j = lax.broadcasted_iota(jnp.int32, (80, MSG), 1)
    picks = [jnp.where((j == i - 20 * p) & (j < 20), 1.0, 0.0).astype(BF) for p in range(4)]
    for q in range(8):
        rows = mm(picks[0], got[4 * q])
        for p in range(1, 4):
            rows = rows + mm(picks[p], got[4 * q + p])
        out[80 * q : 80 * q + 80, :] = rows.astype(BF)
    y, z = ids[3], ids[4]
    own = [got[zh * 16 + y * NZ + z].astype(F32)[24:32] for zh in range(2)]
    out[640:656, :] = jnp.concatenate(own, axis=0).astype(BF)
    for yy in range(NY):
        part = [got[zh * 16 + yy * NZ + z].astype(F32)[32:40] for zh in range(2)]
        out[656 + 16 * yy : 672 + 16 * yy, :] = jnp.concatenate(part, axis=0).astype(BF)


def rank_order(ids, half, first):
    r = lax.broadcasted_iota(jnp.int32, (128, 128), 0)
    j = lax.broadcasted_iota(jnp.int32, (128, 128), 1)
    x, c = ids[0], ids[2]
    k, o = (j >> 5) & 3, (j >> 4) & 1
    zh, h, i = (j >> 3) & 1, (j >> 2) & 1, j & 3
    xs = x ^ k
    rank = (xs * 4 + zh * 2 + (c + o - 2 * c * o)) * 4 + i
    return jnp.where((h == half) & (r == rank + first), 1.0, 0.0).astype(BF)


def fold(a, op):
    out = a[:, 0:128]
    for at in range(128, a.shape[1], 128):
        out = op(out, a[:, at : at + 128])
    return out


def attend_kernel(ids, *refs):
    blocks = refs[:8]
    wq, normed_h, kc_h, vc_h = refs[8:12]
    pieces, lens, ctx = refs[12:16], refs[16], refs[17]
    kv, qs, qa, sn_all, pn_all, oc, normed, lower, merged, kc, vc, sems = refs[18:]
    x, c, y, z = ids[0], ids[2], ids[3], ids[4]
    load = pltpu.make_async_copy(normed_h, normed, sems.at[0])
    caches = [
        pltpu.make_async_copy(kc_h.at[:, y], kc, sems.at[1]),
        pltpu.make_async_copy(vc_h.at[:, y], vc, sems.at[2]),
    ]
    for copy in [load] + caches:
        copy.start()
    stack = jnp.concatenate([b[640:656, :] for b in blocks], axis=0)
    upper = jnp.concatenate(
        [2.0 * mm(rank_order(ids, h, 0), stack) for h in range(2)], axis=1
    ).astype(BF)
    for n in range(8):
        row = ((x ^ (n // 2)) * 4 + c + n % 2 - 2 * c * (n % 2)) * 320
        for zh in range(2):
            to = pl.ds(pl.multiple_of(row + 640 * zh, 320), 320)
            lower[to, :] = blocks[n][zh * 320 : zh * 320 + 320, :]
    for n in range(10):
        rows = slice(n * 512, n * 512 + 512)
        merged[n] = (wq[rows, :].astype(F32) + mm(lower[rows, :], upper)).astype(BF)
    load.wait()
    total = mm(normed[0], merged[0])
    for n in range(1, 10):
        total = total + mm(normed[n], merged[n])
    qs[...] = total.astype(BF).astype(F32)
    for b in range(8):
        pieces_b = [
            qs[s * 64 + b * 8 : s * 64 + b * 8 + 8, h * 128 : h * 128 + 128] for s in range(4) for h in range(2)
        ]
        qa[b * 64 : b * 64 + 64, :] = jnp.concatenate(pieces_b, axis=0).astype(BF)
    for k, ref in enumerate(pieces):
        kv[(z ^ k) & 3] = ref[...]
    key_t = kv[0:2].reshape(128, 256)
    val = kv[2:4].reshape(128, 256).astype(F32).T.astype(BF)
    factor = 1.0 / HD**0.5
    sn_all[...] = mm(qa[...], key_t) * factor
    c8 = lax.broadcasted_iota(jnp.int32, (8, 512), 1)
    r8 = lax.broadcasted_iota(jnp.int32, (8, 512), 0)
    own_cached = (c8 >> 6) == r8
    pos = c8 & 63
    cn = lax.broadcasted_iota(jnp.int32, (64, 256), 1)
    rn = lax.broadcasted_iota(jnp.int32, (64, 256), 0)
    seen = (cn >> 6) <= (rn >> 4)

    for copy in caches:
        copy.wait()

    def batch(b, carry):
        r = pl.multiple_of(b * 8, 8)
        rows = pl.ds(pl.multiple_of(b * 64, 64), 64)
        keys = kc[pl.ds(r, 8)].reshape(512, 128)
        vals = vc[pl.ds(r, 8)].reshape(512, 128)
        length = jnp.zeros((8, 512), jnp.int32)
        for i in range(8):
            length = jnp.where(r8 == i, lens[r + i], length)
        ok = jnp.where(own_cached & (pos < length), 1.0, 0.0)
        okc = jnp.concatenate([ok] * 8, axis=0) > 0.5
        okn = seen & ((cn & 63) == (rn & 7) + r)
        sc = jnp.where(okc, mm_t(qa[rows, :], keys) * factor, -1e30)
        sn = jnp.where(okn, sn_all[rows, :], -1e30)
        top = jnp.max(jnp.maximum(fold(sc, jnp.maximum), fold(sn, jnp.maximum)), axis=1, keepdims=True)
        ec, en = jnp.exp(sc - top), jnp.exp(sn - top)
        total = jnp.sum(fold(ec, jnp.add) + fold(en, jnp.add), axis=1, keepdims=True)
        inverse = 1.0 / total
        pn_all[rows, :] = (en * inverse).astype(BF)
        oc[rows, :] = mm((ec * inverse).astype(BF), vals)
        return carry

    lax.fori_loop(0, 8, batch, 0, unroll=8)
    out = oc[...] + mm(pn_all[...], val)
    for b in range(8):
        for s in range(4):
            for h in range(2):
                n = b * 64 + (s * 2 + h) * 8
                qs[s * 64 + b * 8 : s * 64 + b * 8 + 8, h * 128 : h * 128 + 128] = out[n : n + 8]
    ctx[...] = qs[...].astype(BF)


def merge_o_kernel(ids, *refs):
    blocks = refs[:8]
    wo = refs[8]
    same, other = refs[9:12], refs[12:15]
    out, hold, low, own, sem = refs[15:]
    x, c, y, z = ids[0], ids[2], ids[3], ids[4]
    load = pltpu.make_async_copy(wo.at[:, pl.ds(pl.multiple_of(y * 1280, 1280), 1280)], own, sem)
    load.start()
    ks = x ^ y
    for k in range(4):
        for o in range(2):

            @pl.when(ks == k)
            def _():
                hold[o] = blocks[2 * k + o][0:640, :]

    order = [rank_order(ids, h, 64) for h in range(2)]
    for k in (1, 2, 3, 0):
        if k == 0:
            load.wait()
        yy = (y - k + 4) & 3
        at = pl.multiple_of(656 + 16 * yy, 16)
        stack = jnp.concatenate([b[pl.ds(at, 16), :] for b in blocks], axis=0)
        lower = jnp.concatenate([2.0 * mm(order[h], stack) for h in range(2)], axis=1)
        low[...] = lower.T.astype(BF)
        for zz in range(4):
            zh, cc = zz // 2, zz % 2
            o = c + cc - 2 * c * cc
            u = hold[o, zh * 320 : zh * 320 + 320, :]
            cols = slice(zz * 320, zz * 320 + 320)
            if k == 0:
                out[k, zz ^ z] = (own[:, cols].astype(F32) + mm_t(low[...], u)).astype(BF)
            else:
                for ref, core in ((same[k - 1], c), (other[k - 1], 1 - c)):
                    at = pl.ds(pl.multiple_of(core * 128, 128), 128)
                    out[k, zz ^ z, at] = (ref[:, cols].astype(F32) + mm_t(low[at, :], u)).astype(BF)


def project_kernel(c0, c1, c2, c3, merged, *out):
    for n in (3, 2, 1, 0):
        total = mm(c0[...], merged[0, n])
        for k, ref in ((1, c1), (2, c2), (3, c3)):
            total = total + mm(ref[...], merged[k, n])
        total = total.astype(BF)
        out[n][0:256] = total[:, 0:128]
        out[n][256:512] = total[:, 128:256]
        out[n][512:640] = jnp.concatenate([total[0:128, 256:320], total[128:256, 256:320]], axis=1)


def sum_kernel(p0, p1, p2, p3, out):
    total = p0[...].astype(F32) + p1[...].astype(F32) + p2[...].astype(F32) + p3[...].astype(F32)
    tail = jnp.concatenate([total[512:640, :64], total[512:640, 64:]], axis=0)
    full = jnp.concatenate([total[0:256], total[256:512], tail], axis=1).astype(BF)
    out[...] = full.reshape(out.shape)


def near(a):
    return pltpu.with_memory_space_constraint(a, pltpu.VMEM)


def far(a):
    return pltpu.with_memory_space_constraint(a, pltpu.HBM)


def ring(s):
    return [(i, (i + s) % 4) for i in range(4)]


def partner(s):
    return [(i, i ^ s) for i in range(4)]


def kv_pairs(k):
    pairs = []
    for s in range(16):
        a, e, b = s // 4, (s % 4) // 2, s % 2
        pairs.append((s, (2 * (a % 2) + e) * 4 + (((a // 2) * 2 + b) ^ k)))
    return pairs


def local(states, wq, wkv, wo, qa_low, qa_up, oa_low, oa_up, kcache, vcache, lens):
    x, zh, c, y, z = (lax.axis_index(a) for a in ("x", "zh", "c", "y", "z"))
    ids = jnp.stack([x, zh, c, y, z]).astype(jnp.int32)

    vmem = pl.BlockSpec(memory_space=pltpu.VMEM)
    hbm = pl.BlockSpec(memory_space=pltpu.HBM)

    def array(*shape):
        return jax.ShapeDtypeStruct(shape, BF)

    messages = pl.pallas_call(
        pack_kernel,
        out_shape=array(32, MSG, 128),
        in_specs=[hbm] * 4,
        scratch_shapes=[
            pltpu.VMEM((20, 64), BF),
            pltpu.VMEM((20, 64), BF),
            pltpu.VMEM((4, 256), BF),
            pltpu.VMEM((4, 256), BF),
            pltpu.SemaphoreType.DMA((4,)),
        ],
        compiler_params=params(4),
        name="pack",
    )(*(far(a) for a in (qa_low, oa_up, qa_up, oa_low)))
    got = lax.all_to_all(messages, ("zh", "y", "z"), 0, 0, tiled=True)

    normed, kv_t, *w_sent = pl.pallas_call(
        norm_kernel,
        out_shape=(pltpu.HBM((10, ROWS, 512), BF), array(64, ROWS)) + (pltpu.HBM((128, 1280), BF),) * 3,
        in_specs=[SMEM, hbm, hbm, hbm],
        out_specs=(hbm, vmem, hbm, hbm, hbm),
        scratch_shapes=[
            pltpu.VMEM((STEPS, 64, WIDTH), BF),
            pltpu.VMEM((64, WIDTH), BF),
            pltpu.VMEM((10, ROWS, 512), BF),
            pltpu.VMEM((3, 128, 1280), BF),
            pltpu.SemaphoreType.DMA((15,)),
        ],
        compiler_params=params(20),
        cost_estimate=pl.CostEstimate(flops=170_000_000, bytes_accessed=8_000_000, transcendentals=0),
        name="norm_kv",
    )(ids, far(states), far(wkv.T), far(wo))

    new_kv = [lax.ppermute(kv_t, TP, kv_pairs(k)) for k in range(4)]

    swap = [(0, 1), (1, 0)]
    got, normed, kv_t = lax.optimization_barrier((got, normed, kv_t))
    mine = pl.pallas_call(
        sort_kernel,
        out_shape=array(XROWS, 128),
        in_specs=[SMEM, vmem],
        compiler_params=params(6),
        name="sort_rows",
    )(ids, got)
    mine, w_sent, new_kv = lax.optimization_barrier((mine, w_sent, new_kv))
    w_first = lax.ppermute(w_sent[0], "y", ring(1))
    w_third = lax.ppermute(w_sent[2], "y", ring(3))
    parts = [mine] + [lax.ppermute(mine, "x", partner(s)) for s in (1, 2, 3)]
    w_first, w_third, w_second = lax.optimization_barrier((w_first, w_third, w_sent[1]))
    w_same = [w_first, lax.ppermute(w_second, "y", ring(2)), w_third]
    blocks = []
    for part in parts:
        blocks += [part, lax.ppermute(part, "c", swap)]

    ctx = pl.pallas_call(
        attend_kernel,
        out_shape=array(ROWS, 256),
        in_specs=[SMEM] + [vmem] * 9 + [hbm] * 3 + [vmem] * 4 + [SMEM],
        scratch_shapes=[
            pltpu.VMEM((4, 64, 256), BF),
            pltpu.VMEM((ROWS, 256), F32),
            pltpu.VMEM((512, 128), BF),
            pltpu.VMEM((512, 256), F32),
            pltpu.VMEM((512, 256), BF),
            pltpu.VMEM((512, 128), F32),
            pltpu.VMEM((10, ROWS, 512), BF),
            pltpu.VMEM((WIDTH, 128), BF),
            pltpu.VMEM((10, 512, 256), BF),
            pltpu.VMEM((64, 64, 128), BF),
            pltpu.VMEM((64, 64, 128), BF),
            pltpu.SemaphoreType.DMA((3,)),
        ],
        compiler_params=params(24),
        cost_estimate=pl.CostEstimate(flops=1_000_000_000, bytes_accessed=10_000_000, transcendentals=400_000),
        name="attend",
    )(ids, *blocks, near(wq), far(normed), far(kcache), far(vcache), *new_kv, lens)

    others = {s: lax.ppermute(ctx, "y", ring(s)) for s in (1, 3, 2)}
    _, w_same = lax.optimization_barrier((ctx, w_same))
    w_other = [lax.ppermute(w, "c", swap) for w in w_same]
    merged = pl.pallas_call(
        merge_o_kernel,
        out_shape=array(4, 4, 256, 320),
        in_specs=[SMEM] + [vmem] * 8 + [hbm] + [vmem] * 6,
        scratch_shapes=[
            pltpu.VMEM((2, 640, 128), BF),
            pltpu.VMEM((256, 128), BF),
            pltpu.VMEM((256, 1280), BF),
            pltpu.SemaphoreType.DMA(()),
        ],
        compiler_params=params(20),
        cost_estimate=pl.CostEstimate(flops=340_000_000, bytes_accessed=8_000_000, transcendentals=0),
        name="merge_o",
    )(ids, *blocks, far(wo), *w_same, *w_other)
    sums = pl.pallas_call(
        project_kernel,
        out_shape=(array(640, 128),) * 4,
        compiler_params=params(16),
        cost_estimate=pl.CostEstimate(flops=680_000_000, bytes_accessed=4_000_000, transcendentals=0),
        name="project",
    )(ctx, others[1], others[2], others[3], merged)
    came = [lax.ppermute(sums[n], "z", partner(n)) for n in (3, 2, 1)]
    return pl.pallas_call(
        sum_kernel,
        out_shape=array(4, 64, 320),
        compiler_params=params(6),
        name="sum_parts",
    )(sums[0], *came)


def solution(mesh):
    fine = Mesh(np.asarray(mesh.devices).reshape(NX, NZH, NC, NY, NZ), GROUP + TP)
    every = GROUP + TP
    in_specs = (
        P(None, GROUP, None),
        P(None, TP),
        P(None, TP),
        P(TP, None),
        P(every, None),
        P(GROUP, TP),
        P(GROUP, TP),
        P(every, None),
        P(GROUP, None, None, None),
        P(GROUP, None, None, None),
        P(GROUP),
    )
    out_specs = P(None, GROUP, TP)
    return jax.shard_map(local, mesh=fine, in_specs=in_specs, out_specs=out_specs, check_vma=False)
```

```python
import functools

import jax
import jax.numpy as jnp
import numpy as np
from jax import lax
from jax.experimental import pallas as pl
from jax.experimental.pallas import tpu as pltpu
from jax.sharding import Mesh
from jax.sharding import PartitionSpec as P

HD = 128
STEPS = 4
ROWS = 256
WIDTH = 5120
NX, NZH, NC, NY, NZ = 4, 2, 2, 4, 4
GROUP = ("x", "zh", "c")
TP = ("y", "z")
BF = jnp.bfloat16
F32 = jnp.float32
MSG = 48
ORDER = (0, 3, 2, 1)
XROWS = 720

SMEM = pl.BlockSpec(memory_space=pltpu.SMEM)


def params(mib):
    return pltpu.CompilerParams(vmem_limit_bytes=mib * 1024 * 1024)


def mm(a, b):
    return jnp.dot(a, b, preferred_element_type=F32)


def mm_t(a, b):
    return lax.dot_general(a, b, (((1,), (1,)), ((), ())), preferred_element_type=F32)


def pack_kernel(low, up, q_up, o_low, out):
    def halves(ref):
        a = ref[...].astype(F32)
        return [a[:, :128], a[:, 128:]]

    first = jnp.concatenate([low[...].astype(F32), up[...].astype(F32)], axis=1)
    rows = [first, jnp.zeros((12, 128), F32)] + halves(q_up) + halves(o_low)
    message = jnp.concatenate(rows, axis=0).astype(BF)

    def write(i, carry):
        out[i] = message
        return carry

    lax.fori_loop(0, out.shape[0], write, 0)


def norm_kernel(ids, states, wkv_t, wo, normed_h, kv_t, w1, w2, w3, x_v, w_v, flat, cut, sems):
    c, y = ids[2], ids[3]
    half = pl.ds(pl.multiple_of(c * 128, 128), 128)
    loads = [pltpu.make_async_copy(states.at[n], x_v.at[n], sems.at[n]) for n in range(STEPS)]
    loads.append(pltpu.make_async_copy(wkv_t, w_v, sems.at[STEPS]))
    cuts, puts, stores = [], [], []
    for n, ref in enumerate((w1, w2, w3)):
        at = pl.multiple_of(((y + n + 1) & 3) * 1280, 1280)
        cuts.append(pltpu.make_async_copy(wo.at[half, pl.ds(at, 1280)], cut.at[n], sems.at[5 + n]))
        puts.append(pltpu.make_async_copy(cut.at[n], ref, sems.at[8 + n]))
    for copy in loads + cuts:
        copy.start()
    for n in range(STEPS):
        loads[n].wait()

        def rows(i, carry):
            r = pl.multiple_of(i * 32, 32)
            x = x_v[n, pl.ds(r, 32), :].astype(F32)
            scale = lax.rsqrt(jnp.mean(x * x, axis=1, keepdims=True) + 1e-06)
            normed = (x * scale).astype(BF)
            to = pl.ds(pl.multiple_of(n * 64 + r, 32), 32)
            for k in range(10):
                flat[k, to, :] = normed[:, k * 512 : k * 512 + 512]
            return carry

        lax.fori_loop(0, 2, rows, 0, unroll=True)
        span = pl.ds(n * 64, 64)
        stores.append(pltpu.make_async_copy(flat.at[:, span], normed_h.at[:, span], sems.at[11 + n]))
        stores[n].start()
    for cut_copy, put in zip(cuts, puts):
        cut_copy.wait()
        put.start()
    loads[STEPS].wait()
    total = mm_t(flat[0], w_v[:, 0:512])
    for k in range(1, 10):
        total = total + mm_t(flat[k], w_v[:, k * 512 : k * 512 + 512])
    kv_t[...] = total.T.astype(BF)
    for copy in puts + stores:
        copy.wait()


def sort_kernel(ids, got, out):
    i = lax.broadcasted_iota(jnp.int32, (80, 4 * MSG), 0)
    j = lax.broadcasted_iota(jnp.int32, (80, 4 * MSG), 1)
    hit = i < 0
    for p in range(4):
        hit = hit | ((j - MSG * p == i - 20 * p) & (i >= 20 * p) & (i < 20 * p + 20))
    pick = jnp.where(hit, 1.0, 0.0).astype(BF)
    for q in range(8):
        out[80 * q : 80 * q + 80, :] = mm(pick, got[4 * q : 4 * q + 4].reshape(4 * MSG, 128)).astype(BF)
    y, z = ids[3], ids[4]
    own = [got[zh * 16 + y * NZ + z, 32:48, :].astype(F32)[:8] for zh in range(2)]
    out[640:656, :] = jnp.concatenate(own, axis=0).astype(BF)
    for yy in range(NY):
        part = [got[zh * 16 + yy * NZ + z, 32:48, :].astype(F32)[8:] for zh in range(2)]
        out[656 + 16 * yy : 672 + 16 * yy, :] = jnp.concatenate(part, axis=0).astype(BF)


def rank_order(ids, half, first):
    r = lax.broadcasted_iota(jnp.int32, (128, 128), 0)
    j = lax.broadcasted_iota(jnp.int32, (128, 128), 1)
    x, c = ids[0], ids[2]
    k, o = (j >> 5) & 3, (j >> 4) & 1
    zh, h, i = (j >> 3) & 1, (j >> 2) & 1, j & 3
    xs = x ^ ((4 - k) & 3)
    rank = (xs * 4 + zh * 2 + (c + o - 2 * c * o)) * 4 + i
    return jnp.where((h == half) & (r == rank + first), 1.0, 0.0).astype(BF)


def fold(a, op):
    out = a[:, 0:128]
    for at in range(128, a.shape[1], 128):
        out = op(out, a[:, at : at + 128])
    return out


def attend_kernel(ids, *refs):
    blocks = refs[:8]
    wq, normed_h, kc_h, vc_h = refs[8:12]
    pieces, lens, ctx = refs[12:16], refs[16], refs[17]
    kv, qs, qa, sn_all, pn_all, oc, normed, lower, merged, kc, vc, sems = refs[18:]
    x, c, y, z = ids[0], ids[2], ids[3], ids[4]
    load = pltpu.make_async_copy(normed_h, normed, sems.at[0])
    caches = [
        pltpu.make_async_copy(kc_h.at[:, y], kc, sems.at[1]),
        pltpu.make_async_copy(vc_h.at[:, y], vc, sems.at[2]),
    ]
    for copy in [load] + caches:
        copy.start()
    stack = jnp.concatenate([b[640:656, :] for b in blocks], axis=0)
    upper = jnp.concatenate(
        [2.0 * mm(rank_order(ids, h, 0), stack) for h in range(2)], axis=1
    ).astype(BF)
    for n in range(8):
        row = ((x ^ ORDER[n // 2]) * 4 + c + n % 2 - 2 * c * (n % 2)) * 320
        for zh in range(2):
            to = pl.ds(pl.multiple_of(row + 640 * zh, 320), 320)
            lower[to, :] = blocks[n][zh * 320 : zh * 320 + 320, :]
    for n in range(10):
        rows = slice(n * 512, n * 512 + 512)
        merged[n] = (wq[rows, :].astype(F32) + mm(lower[rows, :], upper)).astype(BF)
    load.wait()
    total = mm(normed[0], merged[0])
    for n in range(1, 10):
        total = total + mm(normed[n], merged[n])
    qs[...] = total.astype(BF).astype(F32)
    for b in range(8):
        pieces_b = [
            qs[s * 64 + b * 8 : s * 64 + b * 8 + 8, h * 128 : h * 128 + 128] for s in range(4) for h in range(2)
        ]
        qa[b * 64 : b * 64 + 64, :] = jnp.concatenate(pieces_b, axis=0).astype(BF)
    for k, ref in enumerate(pieces):
        kv[(z ^ k) & 3] = ref[...]
    key_t = kv[0:2].reshape(128, 256)
    val = kv[2:4].reshape(128, 256).astype(F32).T.astype(BF)
    factor = 1.0 / HD**0.5
    sn_all[...] = mm(qa[...], key_t) * factor
    c8 = lax.broadcasted_iota(jnp.int32, (8, 512), 1)
    r8 = lax.broadcasted_iota(jnp.int32, (8, 512), 0)
    own_cached = (c8 >> 6) == r8
    pos = c8 & 63
    cn = lax.broadcasted_iota(jnp.int32, (64, 256), 1)
    rn = lax.broadcasted_iota(jnp.int32, (64, 256), 0)
    seen = (cn >> 6) <= (rn >> 4)

    for copy in caches:
        copy.wait()

    def batch(b, carry):
        r = pl.multiple_of(b * 8, 8)
        rows = pl.ds(pl.multiple_of(b * 64, 64), 64)
        keys = kc[pl.ds(r, 8)].reshape(512, 128)
        vals = vc[pl.ds(r, 8)].reshape(512, 128)
        length = jnp.zeros((8, 512), jnp.int32)
        for i in range(8):
            length = jnp.where(r8 == i, lens[r + i], length)
        ok = jnp.where(own_cached & (pos < length), 1.0, 0.0)
        okc = jnp.concatenate([ok] * 8, axis=0) > 0.5
        okn = seen & ((cn & 63) == (rn & 7) + r)
        sc = jnp.where(okc, mm_t(qa[rows, :], keys) * factor, -1e30)
        sn = jnp.where(okn, sn_all[rows, :], -1e30)
        top = jnp.max(jnp.maximum(fold(sc, jnp.maximum), fold(sn, jnp.maximum)), axis=1, keepdims=True)
        ec, en = jnp.exp(sc - top), jnp.exp(sn - top)
        total = jnp.sum(fold(ec, jnp.add) + fold(en, jnp.add), axis=1, keepdims=True)
        inverse = 1.0 / total
        pn_all[rows, :] = (en * inverse).astype(BF)
        oc[rows, :] = mm((ec * inverse).astype(BF), vals)
        return carry

    lax.fori_loop(0, 8, batch, 0, unroll=8)
    out = oc[...] + mm(pn_all[...], val)
    for b in range(8):
        for s in range(4):
            for h in range(2):
                n = b * 64 + (s * 2 + h) * 8
                qs[s * 64 + b * 8 : s * 64 + b * 8 + 8, h * 128 : h * 128 + 128] = out[n : n + 8]
    ctx[...] = qs[...].astype(BF)


def merge_o_kernel(ids, *refs):
    blocks = refs[:8]
    wo = refs[8]
    same, other = refs[9:12], refs[12:15]
    out, hold, low, own, sem = refs[15:]
    x, c, y, z = ids[0], ids[2], ids[3], ids[4]
    load = pltpu.make_async_copy(wo.at[:, pl.ds(pl.multiple_of(y * 1280, 1280), 1280)], own, sem)
    load.start()
    ks = x ^ y
    for k in range(4):
        for o in range(2):

            @pl.when(ks == k)
            def _():
                hold[o] = blocks[2 * ORDER[k] + o][0:640, :]

    order = [rank_order(ids, h, 64) for h in range(2)]
    for k in (1, 2, 3, 0):
        if k == 0:
            load.wait()
        yy = (y - k + 4) & 3
        at = pl.multiple_of(656 + 16 * yy, 16)
        stack = jnp.concatenate([b[pl.ds(at, 16), :] for b in blocks], axis=0)
        lower = jnp.concatenate([2.0 * mm(order[h], stack) for h in range(2)], axis=1)
        low[...] = lower.T.astype(BF)
        for zz in range(4):
            zh, cc = zz // 2, zz % 2
            o = c + cc - 2 * c * cc
            u = hold[o, zh * 320 : zh * 320 + 320, :]
            cols = slice(zz * 320, zz * 320 + 320)
            if k == 0:
                out[k, zz ^ z] = (own[:, cols].astype(F32) + mm_t(low[...], u)).astype(BF)
            else:
                for ref, core in ((same[k - 1], c), (other[k - 1], 1 - c)):
                    at = pl.ds(pl.multiple_of(core * 128, 128), 128)
                    out[k, zz ^ z, at] = (ref[:, cols].astype(F32) + mm_t(low[at, :], u)).astype(BF)


def project_kernel(order, c0, c1, c3, c2, merged, *out):
    for n, ref_out in zip(order, out):
        total = mm(c0[...], merged[0, n])
        for k, ref in ((1, c1), (2, c2), (3, c3)):
            total = total + mm(ref[...], merged[k, n])
        total = total.astype(BF)
        ref_out[0:256] = total[:, 0:128]
        ref_out[256:512] = total[:, 128:256]
        ref_out[512:640] = jnp.concatenate([total[0:128, 256:320], total[128:256, 256:320]], axis=1)


def sum_kernel(p0, p1, p2, p3, out):
    total = p0[...].astype(F32) + p1[...].astype(F32) + p2[...].astype(F32) + p3[...].astype(F32)
    tail = jnp.concatenate([total[512:640, :64], total[512:640, 64:]], axis=0)
    full = jnp.concatenate([total[0:256], total[256:512], tail], axis=1).astype(BF)
    out[...] = full.reshape(out.shape)


def near(a):
    return pltpu.with_memory_space_constraint(a, pltpu.VMEM)


def far(a):
    return pltpu.with_memory_space_constraint(a, pltpu.HBM)


def ring(s):
    return [(i, (i + s) % 4) for i in range(4)]


def partner(s):
    return [(i, i ^ s) for i in range(4)]


def kv_pairs(k):
    pairs = []
    for s in range(16):
        a, e, b = s // 4, (s % 4) // 2, s % 2
        pairs.append((s, (2 * (a % 2) + e) * 4 + (((a // 2) * 2 + b) ^ k)))
    return pairs


def local(states, wq, wkv, wo, qa_low, qa_up, oa_low, oa_up, kcache, vcache, lens):
    x, zh, c, y, z = (lax.axis_index(a) for a in ("x", "zh", "c", "y", "z"))
    ids = jnp.stack([x, zh, c, y, z]).astype(jnp.int32)

    vmem = pl.BlockSpec(memory_space=pltpu.VMEM)
    hbm = pl.BlockSpec(memory_space=pltpu.HBM)

    def array(*shape):
        return jax.ShapeDtypeStruct(shape, BF)

    messages = pl.pallas_call(
        pack_kernel,
        out_shape=array(32, MSG, 128),
        compiler_params=params(4),
        name="pack",
    )(*(far(a) for a in (qa_low, oa_up, qa_up, oa_low)))
    got = lax.all_to_all(messages, ("zh", "y", "z"), 0, 0, tiled=True)

    normed, kv_t, *w_sent = pl.pallas_call(
        norm_kernel,
        out_shape=(pltpu.HBM((10, ROWS, 512), BF), array(64, ROWS)) + (pltpu.HBM((128, 1280), BF),) * 3,
        in_specs=[SMEM, hbm, hbm, hbm],
        out_specs=(hbm, vmem, hbm, hbm, hbm),
        scratch_shapes=[
            pltpu.VMEM((STEPS, 64, WIDTH), BF),
            pltpu.VMEM((64, WIDTH), BF),
            pltpu.VMEM((10, ROWS, 512), BF),
            pltpu.VMEM((3, 128, 1280), BF),
            pltpu.SemaphoreType.DMA((15,)),
        ],
        compiler_params=params(20),
        cost_estimate=pl.CostEstimate(flops=170_000_000, bytes_accessed=8_000_000, transcendentals=0),
        name="norm_kv",
    )(ids, far(states), far(wkv.T), far(wo))

    new_kv = [lax.ppermute(kv_t, TP, kv_pairs(k)) for k in range(4)]

    swap = [(0, 1), (1, 0)]
    got, normed, kv_t = lax.optimization_barrier((got, normed, kv_t))
    mine = pl.pallas_call(
        sort_kernel,
        out_shape=array(XROWS, 128),
        in_specs=[SMEM, vmem],
        compiler_params=params(6),
        name="sort_rows",
    )(ids, got)
    mine, w_sent, new_kv = lax.optimization_barrier((mine, w_sent, new_kv))
    w_first = lax.ppermute(w_sent[0], "y", ring(1))
    w_third = lax.ppermute(w_sent[2], "y", ring(3))
    parts = [mine] + [lax.ppermute(mine, "x", partner(s)) for s in ORDER[1:]]
    w_first, w_third, w_second = lax.optimization_barrier((w_first, w_third, w_sent[1]))
    w_same = [w_first, lax.ppermute(w_second, "y", ring(2)), w_third]
    blocks = []
    for part in parts:
        blocks += [part, lax.ppermute(part, "c", swap)]

    ctx = pl.pallas_call(
        attend_kernel,
        out_shape=array(ROWS, 256),
        in_specs=[SMEM] + [vmem] * 9 + [hbm] * 3 + [vmem] * 4 + [SMEM],
        scratch_shapes=[
            pltpu.VMEM((4, 64, 256), BF),
            pltpu.VMEM((ROWS, 256), F32),
            pltpu.VMEM((512, 128), BF),
            pltpu.VMEM((512, 256), F32),
            pltpu.VMEM((512, 256), BF),
            pltpu.VMEM((512, 128), F32),
            pltpu.VMEM((10, ROWS, 512), BF),
            pltpu.VMEM((WIDTH, 128), BF),
            pltpu.VMEM((10, 512, 256), BF),
            pltpu.VMEM((64, 64, 128), BF),
            pltpu.VMEM((64, 64, 128), BF),
            pltpu.SemaphoreType.DMA((3,)),
        ],
        compiler_params=params(24),
        cost_estimate=pl.CostEstimate(flops=1_000_000_000, bytes_accessed=10_000_000, transcendentals=400_000),
        name="attend",
    )(ids, *blocks, near(wq), far(normed), far(kcache), far(vcache), *new_kv, lens)

    others = {s: lax.ppermute(ctx, "y", ring(s)) for s in (1, 3, 2)}
    _, w_same = lax.optimization_barrier((ctx, w_same))
    w_other = [lax.ppermute(w, "c", swap) for w in w_same]
    merged = pl.pallas_call(
        merge_o_kernel,
        out_shape=array(4, 4, 256, 320),
        in_specs=[SMEM] + [vmem] * 8 + [hbm] + [vmem] * 6,
        scratch_shapes=[
            pltpu.VMEM((2, 640, 128), BF),
            pltpu.VMEM((256, 128), BF),
            pltpu.VMEM((256, 1280), BF),
            pltpu.SemaphoreType.DMA(()),
        ],
        compiler_params=params(20),
        cost_estimate=pl.CostEstimate(flops=340_000_000, bytes_accessed=8_000_000, transcendentals=0),
        name="merge_o",
    )(ids, *blocks, far(wo), *w_same, *w_other)
    sums = {}
    for order in ((2, 1), (3, 0)):
        both = pl.pallas_call(
            functools.partial(project_kernel, order),
            out_shape=(array(640, 128),) * 2,
            compiler_params=params(16),
            cost_estimate=pl.CostEstimate(flops=340_000_000, bytes_accessed=4_000_000, transcendentals=0),
            name="project",
        )(ctx, others[1], others[3], others[2], merged)
        sums.update(zip(order, both))
    came = [lax.ppermute(sums[n], "z", partner(n)) for n in (2, 1, 3)]
    return pl.pallas_call(
        sum_kernel,
        out_shape=array(4, 64, 320),
        compiler_params=params(6),
        name="sum_parts",
    )(sums[0], *came)


def solution(mesh):
    fine = Mesh(np.asarray(mesh.devices).reshape(NX, NZH, NC, NY, NZ), GROUP + TP)
    every = GROUP + TP
    in_specs = (
        P(None, GROUP, None),
        P(None, TP),
        P(None, TP),
        P(TP, None),
        P(every, None),
        P(GROUP, TP),
        P(GROUP, TP),
        P(every, None),
        P(GROUP, None, None, None),
        P(GROUP, None, None, None),
        P(GROUP),
    )
    out_specs = P(None, GROUP, TP)
    return jax.shard_map(local, mesh=fine, in_specs=in_specs, out_specs=out_specs, check_vma=False)
```

```python
import functools

import jax
import jax.numpy as jnp
import numpy as np
from jax import lax
from jax.experimental import pallas as pl
from jax.experimental.pallas import tpu as pltpu
from jax.sharding import Mesh
from jax.sharding import PartitionSpec as P

HD = 128
STEPS = 4
ROWS = 256
WIDTH = 5120
NX, NZH, NC, NY, NZ = 4, 2, 2, 4, 4
GROUP = ("x", "zh", "c")
TP = ("y", "z")
BF = jnp.bfloat16
F32 = jnp.float32
MSG = 48
ORDER = (0, 3, 2, 1)
XROWS = 720

SMEM = pl.BlockSpec(memory_space=pltpu.SMEM)


def params(mib):
    return pltpu.CompilerParams(vmem_limit_bytes=mib * 1024 * 1024)


def mm(a, b):
    return jnp.dot(a, b, preferred_element_type=F32)


def mm_t(a, b):
    return lax.dot_general(a, b, (((1,), (1,)), ((), ())), preferred_element_type=F32)


def pack_kernel(low, up, q_up, o_low, out):
    def halves(ref):
        a = ref[...].astype(F32)
        return [a[:, :128], a[:, 128:]]

    first = jnp.concatenate([low[...].astype(F32), up[...].astype(F32)], axis=1)
    rows = [first, jnp.zeros((12, 128), F32)] + halves(q_up) + halves(o_low)
    message = jnp.concatenate(rows, axis=0).astype(BF)

    def write(i, carry):
        out[i] = message
        return carry

    lax.fori_loop(0, out.shape[0], write, 0)


def norm_kernel(ids, states, wkv_t, wo, normed_h, kv_t, w1, w2, w3, x_v, w_v, flat, cut, sems):
    c, y = ids[2], ids[3]
    half = pl.ds(pl.multiple_of(c * 128, 128), 128)
    loads = [pltpu.make_async_copy(states.at[n], x_v.at[n], sems.at[n]) for n in range(STEPS)]
    loads.append(pltpu.make_async_copy(wkv_t, w_v, sems.at[STEPS]))
    cuts, puts, stores = [], [], []
    for n, ref in enumerate((w1, w2, w3)):
        at = pl.multiple_of(((y + n + 1) & 3) * 1280, 1280)
        cuts.append(pltpu.make_async_copy(wo.at[half, pl.ds(at, 1280)], cut.at[n], sems.at[5 + n]))
        puts.append(pltpu.make_async_copy(cut.at[n], ref, sems.at[8 + n]))
    for copy in loads + cuts:
        copy.start()
    for n in range(STEPS):
        loads[n].wait()

        def rows(i, carry):
            r = pl.multiple_of(i * 32, 32)
            x = x_v[n, pl.ds(r, 32), :].astype(F32)
            scale = lax.rsqrt(jnp.mean(x * x, axis=1, keepdims=True) + 1e-06)
            normed = (x * scale).astype(BF)
            to = pl.ds(pl.multiple_of(n * 64 + r, 32), 32)
            for k in range(10):
                flat[k, to, :] = normed[:, k * 512 : k * 512 + 512]
            return carry

        lax.fori_loop(0, 2, rows, 0, unroll=True)
        span = pl.ds(n * 64, 64)
        stores.append(pltpu.make_async_copy(flat.at[:, span], normed_h.at[:, span], sems.at[11 + n]))
        stores[n].start()
    for cut_copy, put in zip(cuts, puts):
        cut_copy.wait()
        put.start()
    loads[STEPS].wait()
    total = mm_t(flat[0], w_v[:, 0:512])
    for k in range(1, 10):
        total = total + mm_t(flat[k], w_v[:, k * 512 : k * 512 + 512])
    kv_t[...] = total.T.astype(BF)
    for copy in puts + stores:
        copy.wait()


def sort_kernel(ids, got, out):
    i = lax.broadcasted_iota(jnp.int32, (80, 4 * MSG), 0)
    j = lax.broadcasted_iota(jnp.int32, (80, 4 * MSG), 1)
    hit = i < 0
    for p in range(4):
        hit = hit | ((j - MSG * p == i - 20 * p) & (i >= 20 * p) & (i < 20 * p + 20))
    pick = jnp.where(hit, 1.0, 0.0).astype(BF)
    for q in range(8):
        out[80 * q : 80 * q + 80, :] = mm(pick, got[4 * q : 4 * q + 4].reshape(4 * MSG, 128)).astype(BF)
    y, z = ids[3], ids[4]
    own = [got[zh * 16 + y * NZ + z, 32:48, :].astype(F32)[:8] for zh in range(2)]
    out[640:656, :] = jnp.concatenate(own, axis=0).astype(BF)
    for yy in range(NY):
        part = [got[zh * 16 + yy * NZ + z, 32:48, :].astype(F32)[8:] for zh in range(2)]
        out[656 + 16 * yy : 672 + 16 * yy, :] = jnp.concatenate(part, axis=0).astype(BF)


def rank_order(ids, half, first):
    r = lax.broadcasted_iota(jnp.int32, (128, 128), 0)
    j = lax.broadcasted_iota(jnp.int32, (128, 128), 1)
    x, c = ids[0], ids[2]
    k, o = (j >> 5) & 3, (j >> 4) & 1
    zh, h, i = (j >> 3) & 1, (j >> 2) & 1, j & 3
    xs = x ^ ((4 - k) & 3)
    rank = (xs * 4 + zh * 2 + (c + o - 2 * c * o)) * 4 + i
    return jnp.where((h == half) & (r == rank + first), 1.0, 0.0).astype(BF)


def fold(a, op):
    out = a[:, 0:128]
    for at in range(128, a.shape[1], 128):
        out = op(out, a[:, at : at + 128])
    return out


def attend_kernel(ids, *refs):
    blocks = refs[:8]
    wq, normed_h, kc_h, vc_h = refs[8:12]
    pieces, lens, ctx = refs[12:16], refs[16], refs[17]
    kv, qs, qa, sn_all, pn_all, oc, normed, lower, merged, kc, vc, sems = refs[18:]
    x, c, y, z = ids[0], ids[2], ids[3], ids[4]
    load = pltpu.make_async_copy(normed_h, normed, sems.at[0])
    caches = [
        pltpu.make_async_copy(kc_h.at[:, y], kc, sems.at[1]),
        pltpu.make_async_copy(vc_h.at[:, y], vc, sems.at[2]),
    ]
    for copy in [load] + caches:
        copy.start()
    stack = jnp.concatenate([b[640:656, :] for b in blocks], axis=0)
    upper = jnp.concatenate(
        [2.0 * mm(rank_order(ids, h, 0), stack) for h in range(2)], axis=1
    ).astype(BF)
    for n in range(8):
        row = ((x ^ ORDER[n // 2]) * 4 + c + n % 2 - 2 * c * (n % 2)) * 320
        for zh in range(2):
            to = pl.ds(pl.multiple_of(row + 640 * zh, 320), 320)
            lower[to, :] = blocks[n][zh * 320 : zh * 320 + 320, :]
    for n in range(10):
        rows = slice(n * 512, n * 512 + 512)
        merged[n] = (wq[rows, :].astype(F32) + mm(lower[rows, :], upper)).astype(BF)
    load.wait()
    total = mm(normed[0], merged[0])
    for n in range(1, 10):
        total = total + mm(normed[n], merged[n])
    qs[...] = total.astype(BF).astype(F32)
    for b in range(8):
        pieces_b = [
            qs[s * 64 + b * 8 : s * 64 + b * 8 + 8, h * 128 : h * 128 + 128] for s in range(4) for h in range(2)
        ]
        qa[b * 64 : b * 64 + 64, :] = jnp.concatenate(pieces_b, axis=0).astype(BF)
    for k, ref in enumerate(pieces):
        kv[(z ^ k) & 3] = ref[...]
    key_t = kv[0:2].reshape(128, 256)
    val = kv[2:4].reshape(128, 256).astype(F32).T.astype(BF)
    factor = 1.0 / HD**0.5
    sn_all[...] = mm(qa[...], key_t) * factor
    c8 = lax.broadcasted_iota(jnp.int32, (8, 512), 1)
    r8 = lax.broadcasted_iota(jnp.int32, (8, 512), 0)
    own_cached = (c8 >> 6) == r8
    pos = c8 & 63
    cn = lax.broadcasted_iota(jnp.int32, (64, 256), 1)
    rn = lax.broadcasted_iota(jnp.int32, (64, 256), 0)
    seen = (cn >> 6) <= (rn >> 4)

    for copy in caches:
        copy.wait()

    def batch(b, carry):
        r = pl.multiple_of(b * 8, 8)
        rows = pl.ds(pl.multiple_of(b * 64, 64), 64)
        keys = kc[pl.ds(r, 8)].reshape(512, 128)
        vals = vc[pl.ds(r, 8)].reshape(512, 128)
        length = jnp.zeros((8, 512), jnp.int32)
        for i in range(8):
            length = jnp.where(r8 == i, lens[r + i], length)
        ok = jnp.where(own_cached & (pos < length), 1.0, 0.0)
        okc = jnp.concatenate([ok] * 8, axis=0) > 0.5
        okn = seen & ((cn & 63) == (rn & 7) + r)
        sc = jnp.where(okc, mm_t(qa[rows, :], keys) * factor, -1e30)
        sn = jnp.where(okn, sn_all[rows, :], -1e30)
        top = jnp.max(jnp.maximum(fold(sc, jnp.maximum), fold(sn, jnp.maximum)), axis=1, keepdims=True)
        ec, en = jnp.exp(sc - top), jnp.exp(sn - top)
        total = jnp.sum(fold(ec, jnp.add) + fold(en, jnp.add), axis=1, keepdims=True)
        inverse = 1.0 / total
        pn_all[rows, :] = (en * inverse).astype(BF)
        oc[rows, :] = mm((ec * inverse).astype(BF), vals)
        return carry

    lax.fori_loop(0, 8, batch, 0, unroll=8)
    out = oc[...] + mm(pn_all[...], val)
    for b in range(8):
        for s in range(4):
            for h in range(2):
                n = b * 64 + (s * 2 + h) * 8
                qs[s * 64 + b * 8 : s * 64 + b * 8 + 8, h * 128 : h * 128 + 128] = out[n : n + 8]
    ctx[...] = qs[...].astype(BF)


def merge_o_kernel(ids, *refs):
    blocks = refs[:8]
    wo = refs[8]
    same, other = refs[9:12], refs[12:15]
    out, hold, low, own, sem = refs[15:]
    x, c, y, z = ids[0], ids[2], ids[3], ids[4]
    load = pltpu.make_async_copy(wo.at[:, pl.ds(pl.multiple_of(y * 1280, 1280), 1280)], own, sem)
    load.start()
    ks = x ^ y
    for k in range(4):
        for o in range(2):

            @pl.when(ks == k)
            def _():
                hold[o] = blocks[2 * ORDER[k] + o][0:640, :]

    order = [rank_order(ids, h, 64) for h in range(2)]
    for k in (1, 2, 3, 0):
        if k == 0:
            load.wait()
        yy = (y - k + 4) & 3
        at = pl.multiple_of(656 + 16 * yy, 16)
        stack = jnp.concatenate([b[pl.ds(at, 16), :] for b in blocks], axis=0)
        lower = jnp.concatenate([2.0 * mm(order[h], stack) for h in range(2)], axis=1)
        low[...] = lower.T.astype(BF)
        for zz in range(4):
            zh, cc = zz // 2, zz % 2
            o = c + cc - 2 * c * cc
            u = hold[o, zh * 320 : zh * 320 + 320, :]
            cols = slice(zz * 320, zz * 320 + 320)
            if k == 0:
                out[k, zz ^ z] = (own[:, cols].astype(F32) + mm_t(low[...], u)).astype(BF)
            else:
                for ref, core in ((same[k - 1], c), (other[k - 1], 1 - c)):
                    at = pl.ds(pl.multiple_of(core * 128, 128), 128)
                    out[k, zz ^ z, at] = (ref[:, cols].astype(F32) + mm_t(low[at, :], u)).astype(BF)


def begin_kernel(c0, c1, merged, out):
    for n in range(4):
        out[n] = mm(c0[...], merged[0, n]) + mm(c1[...], merged[1, n])


def project_kernel(order, c3, c2, merged, begun, *out):
    for n, ref_out in zip(order, out):
        total = begun[n] + mm(c3[...], merged[3, n]) + mm(c2[...], merged[2, n])
        total = total.astype(BF)
        ref_out[0:256] = total[:, 0:128]
        ref_out[256:512] = total[:, 128:256]
        ref_out[512:640] = jnp.concatenate([total[0:128, 256:320], total[128:256, 256:320]], axis=1)


def sum_kernel(p0, p1, p2, p3, out):
    total = p0[...].astype(F32) + p1[...].astype(F32) + p2[...].astype(F32) + p3[...].astype(F32)
    tail = jnp.concatenate([total[512:640, :64], total[512:640, 64:]], axis=0)
    full = jnp.concatenate([total[0:256], total[256:512], tail], axis=1).astype(BF)
    out[...] = full.reshape(out.shape)


def near(a):
    return pltpu.with_memory_space_constraint(a, pltpu.VMEM)


def far(a):
    return pltpu.with_memory_space_constraint(a, pltpu.HBM)


def ring(s):
    return [(i, (i + s) % 4) for i in range(4)]


def partner(s):
    return [(i, i ^ s) for i in range(4)]


def kv_pairs(k):
    pairs = []
    for s in range(16):
        a, e, b = s // 4, (s % 4) // 2, s % 2
        pairs.append((s, (2 * (a % 2) + e) * 4 + (((a // 2) * 2 + b) ^ k)))
    return pairs


def local(states, wq, wkv, wo, qa_low, qa_up, oa_low, oa_up, kcache, vcache, lens):
    x, zh, c, y, z = (lax.axis_index(a) for a in ("x", "zh", "c", "y", "z"))
    ids = jnp.stack([x, zh, c, y, z]).astype(jnp.int32)

    vmem = pl.BlockSpec(memory_space=pltpu.VMEM)
    hbm = pl.BlockSpec(memory_space=pltpu.HBM)

    def array(*shape):
        return jax.ShapeDtypeStruct(shape, BF)

    messages = pl.pallas_call(
        pack_kernel,
        out_shape=array(32, MSG, 128),
        compiler_params=params(4),
        name="pack",
    )(*(far(a) for a in (qa_low, oa_up, qa_up, oa_low)))
    got = lax.all_to_all(messages, ("zh", "y", "z"), 0, 0, tiled=True)

    normed, kv_t, *w_sent = pl.pallas_call(
        norm_kernel,
        out_shape=(pltpu.HBM((10, ROWS, 512), BF), array(64, ROWS)) + (pltpu.HBM((128, 1280), BF),) * 3,
        in_specs=[SMEM, hbm, hbm, hbm],
        out_specs=(hbm, vmem, hbm, hbm, hbm),
        scratch_shapes=[
            pltpu.VMEM((STEPS, 64, WIDTH), BF),
            pltpu.VMEM((64, WIDTH), BF),
            pltpu.VMEM((10, ROWS, 512), BF),
            pltpu.VMEM((3, 128, 1280), BF),
            pltpu.SemaphoreType.DMA((15,)),
        ],
        compiler_params=params(20),
        cost_estimate=pl.CostEstimate(flops=170_000_000, bytes_accessed=8_000_000, transcendentals=0),
        name="norm_kv",
    )(ids, far(states), far(wkv.T), far(wo))

    new_kv = [lax.ppermute(kv_t, TP, kv_pairs(k)) for k in range(4)]

    swap = [(0, 1), (1, 0)]
    got, normed, kv_t = lax.optimization_barrier((got, normed, kv_t))
    mine = pl.pallas_call(
        sort_kernel,
        out_shape=array(XROWS, 128),
        in_specs=[SMEM, vmem],
        compiler_params=params(6),
        name="sort_rows",
    )(ids, got)
    mine, w_sent, new_kv = lax.optimization_barrier((mine, w_sent, new_kv))
    w_first = lax.ppermute(w_sent[0], "y", ring(1))
    w_third = lax.ppermute(w_sent[2], "y", ring(3))
    parts = [mine] + [lax.ppermute(mine, "x", partner(s)) for s in ORDER[1:]]
    w_first, w_third, w_second = lax.optimization_barrier((w_first, w_third, w_sent[1]))
    w_same = [w_first, lax.ppermute(w_second, "y", ring(2)), w_third]
    blocks = []
    for part in parts:
        blocks += [part, lax.ppermute(part, "c", swap)]

    ctx = pl.pallas_call(
        attend_kernel,
        out_shape=array(ROWS, 256),
        in_specs=[SMEM] + [vmem] * 9 + [hbm] * 3 + [vmem] * 4 + [SMEM],
        scratch_shapes=[
            pltpu.VMEM((4, 64, 256), BF),
            pltpu.VMEM((ROWS, 256), F32),
            pltpu.VMEM((512, 128), BF),
            pltpu.VMEM((512, 256), F32),
            pltpu.VMEM((512, 256), BF),
            pltpu.VMEM((512, 128), F32),
            pltpu.VMEM((10, ROWS, 512), BF),
            pltpu.VMEM((WIDTH, 128), BF),
            pltpu.VMEM((10, 512, 256), BF),
            pltpu.VMEM((64, 64, 128), BF),
            pltpu.VMEM((64, 64, 128), BF),
            pltpu.SemaphoreType.DMA((3,)),
        ],
        compiler_params=params(24),
        cost_estimate=pl.CostEstimate(flops=1_000_000_000, bytes_accessed=10_000_000, transcendentals=400_000),
        name="attend",
    )(ids, *blocks, near(wq), far(normed), far(kcache), far(vcache), *new_kv, lens)

    others = {s: lax.ppermute(ctx, "y", ring(s)) for s in (1, 3, 2)}
    _, w_same = lax.optimization_barrier((ctx, w_same))
    w_other = [lax.ppermute(w, "c", swap) for w in w_same]
    merged = pl.pallas_call(
        merge_o_kernel,
        out_shape=array(4, 4, 256, 320),
        in_specs=[SMEM] + [vmem] * 8 + [hbm] + [vmem] * 6,
        scratch_shapes=[
            pltpu.VMEM((2, 640, 128), BF),
            pltpu.VMEM((256, 128), BF),
            pltpu.VMEM((256, 1280), BF),
            pltpu.SemaphoreType.DMA(()),
        ],
        compiler_params=params(20),
        cost_estimate=pl.CostEstimate(flops=340_000_000, bytes_accessed=8_000_000, transcendentals=0),
        name="merge_o",
    )(ids, *blocks, far(wo), *w_same, *w_other)
    begun = pl.pallas_call(
        begin_kernel,
        out_shape=jax.ShapeDtypeStruct((4, ROWS, 320), F32),
        compiler_params=params(16),
        cost_estimate=pl.CostEstimate(flops=340_000_000, bytes_accessed=4_000_000, transcendentals=0),
        name="begin",
    )(ctx, others[1], merged)
    sums = {}
    for order in ((2, 1), (3, 0)):
        both = pl.pallas_call(
            functools.partial(project_kernel, order),
            out_shape=(array(640, 128),) * 2,
            compiler_params=params(16),
            cost_estimate=pl.CostEstimate(flops=340_000_000, bytes_accessed=4_000_000, transcendentals=0),
            name="project",
        )(others[3], others[2], merged, begun)
        sums.update(zip(order, both))
    came = [lax.ppermute(sums[n], "z", partner(n)) for n in (2, 1, 3)]
    return pl.pallas_call(
        sum_kernel,
        out_shape=array(4, 64, 320),
        compiler_params=params(6),
        name="sum_parts",
    )(sums[0], *came)


def solution(mesh):
    fine = Mesh(np.asarray(mesh.devices).reshape(NX, NZH, NC, NY, NZ), GROUP + TP)
    every = GROUP + TP
    in_specs = (
        P(None, GROUP, None),
        P(None, TP),
        P(None, TP),
        P(TP, None),
        P(every, None),
        P(GROUP, TP),
        P(GROUP, TP),
        P(every, None),
        P(GROUP, None, None, None),
        P(GROUP, None, None, None),
        P(GROUP),
    )
    out_specs = P(None, GROUP, TP)
    return jax.shard_map(local, mesh=fine, in_specs=in_specs, out_specs=out_specs, check_vma=False)
```

```python
import functools

import jax
import jax.numpy as jnp
import numpy as np
from jax import lax
from jax.experimental import pallas as pl
from jax.experimental.pallas import tpu as pltpu
from jax.sharding import Mesh
from jax.sharding import PartitionSpec as P

HD = 128
STEPS = 4
ROWS = 256
WIDTH = 5120
NX, NZH, NC, NY, NZ = 4, 2, 2, 4, 4
GROUP = ("x", "zh", "c")
TP = ("y", "z")
BF = jnp.bfloat16
F32 = jnp.float32
MSG = 48
ORDER = (0, 3, 2, 1)
XROWS = 720

SMEM = pl.BlockSpec(memory_space=pltpu.SMEM)


def params(mib):
    return pltpu.CompilerParams(vmem_limit_bytes=mib * 1024 * 1024)


def mm(a, b):
    return jnp.dot(a, b, preferred_element_type=F32)


def mm_t(a, b):
    return lax.dot_general(a, b, (((1,), (1,)), ((), ())), preferred_element_type=F32)


def pack_kernel(low, up, q_up, o_low, out):
    def halves(ref):
        a = ref[...].astype(F32)
        return [a[:, :128], a[:, 128:]]

    first = jnp.concatenate([low[...].astype(F32), up[...].astype(F32)], axis=1)
    rows = [first, jnp.zeros((12, 128), F32)] + halves(q_up) + halves(o_low)
    message = jnp.concatenate(rows, axis=0).astype(BF)

    def write(i, carry):
        out[i] = message
        return carry

    lax.fori_loop(0, out.shape[0], write, 0)


def norm_kernel(ids, states, wkv_t, wo, normed_h, kv_t, w1, w2, w3, x_v, w_v, flat, cut, sems):
    c, y = ids[2], ids[3]
    half = pl.ds(pl.multiple_of(c * 128, 128), 128)
    loads = [pltpu.make_async_copy(states.at[n], x_v.at[n], sems.at[n]) for n in range(STEPS)]
    loads.append(pltpu.make_async_copy(wkv_t, w_v, sems.at[STEPS]))
    cuts, puts, stores = [], [], []
    for n, ref in enumerate((w1, w2, w3)):
        at = pl.multiple_of(((y + n + 1) & 3) * 1280, 1280)
        cuts.append(pltpu.make_async_copy(wo.at[half, pl.ds(at, 1280)], cut.at[n], sems.at[5 + n]))
        puts.append(pltpu.make_async_copy(cut.at[n], ref, sems.at[8 + n]))
    for copy in loads + cuts:
        copy.start()
    for n in range(STEPS):
        loads[n].wait()

        def rows(i, carry):
            r = pl.multiple_of(i * 32, 32)
            x = x_v[n, pl.ds(r, 32), :].astype(F32)
            scale = lax.rsqrt(jnp.mean(x * x, axis=1, keepdims=True) + 1e-06)
            normed = (x * scale).astype(BF)
            to = pl.ds(pl.multiple_of(n * 64 + r, 32), 32)
            for k in range(10):
                flat[k, to, :] = normed[:, k * 512 : k * 512 + 512]
            return carry

        lax.fori_loop(0, 2, rows, 0, unroll=True)
        span = pl.ds(n * 64, 64)
        stores.append(pltpu.make_async_copy(flat.at[:, span], normed_h.at[:, span], sems.at[11 + n]))
        stores[n].start()
    for cut_copy, put in zip(cuts, puts):
        cut_copy.wait()
        put.start()
    loads[STEPS].wait()
    total = mm_t(flat[0], w_v[:, 0:512])
    for k in range(1, 10):
        total = total + mm_t(flat[k], w_v[:, k * 512 : k * 512 + 512])
    kv_t[...] = total.T.astype(BF)
    for copy in puts + stores:
        copy.wait()


def sort_kernel(ids, got, out):
    i = lax.broadcasted_iota(jnp.int32, (80, 4 * MSG), 0)
    j = lax.broadcasted_iota(jnp.int32, (80, 4 * MSG), 1)
    hit = i < 0
    for p in range(4):
        hit = hit | ((j - MSG * p == i - 20 * p) & (i >= 20 * p) & (i < 20 * p + 20))
    pick = jnp.where(hit, 1.0, 0.0).astype(BF)
    for q in range(8):
        out[80 * q : 80 * q + 80, :] = mm(pick, got[4 * q : 4 * q + 4].reshape(4 * MSG, 128)).astype(BF)
    y, z = ids[3], ids[4]
    own = [got[zh * 16 + y * NZ + z, 32:48, :].astype(F32)[:8] for zh in range(2)]
    out[640:656, :] = jnp.concatenate(own, axis=0).astype(BF)
    for yy in range(NY):
        part = [got[zh * 16 + yy * NZ + z, 32:48, :].astype(F32)[8:] for zh in range(2)]
        out[656 + 16 * yy : 672 + 16 * yy, :] = jnp.concatenate(part, axis=0).astype(BF)


def rank_order(ids, half, first):
    r = lax.broadcasted_iota(jnp.int32, (128, 128), 0)
    j = lax.broadcasted_iota(jnp.int32, (128, 128), 1)
    x, c = ids[0], ids[2]
    k, o = (j >> 5) & 3, (j >> 4) & 1
    zh, h, i = (j >> 3) & 1, (j >> 2) & 1, j & 3
    xs = x ^ ((4 - k) & 3)
    rank = (xs * 4 + zh * 2 + (c + o - 2 * c * o)) * 4 + i
    return jnp.where((h == half) & (r == rank + first), 1.0, 0.0).astype(BF)


def fold(a, op):
    out = a[:, 0:128]
    for at in range(128, a.shape[1], 128):
        out = op(out, a[:, at : at + 128])
    return out


def attend_kernel(ids, *refs):
    blocks = refs[:8]
    wq, normed_h, kc_h, vc_h = refs[8:12]
    pieces, lens, ctx = refs[12:16], refs[16], refs[17]
    kv, qs, qa, sn_all, pn_all, oc, normed, lower, merged, kc, vc, sems = refs[18:]
    x, c, y, z = ids[0], ids[2], ids[3], ids[4]
    load = pltpu.make_async_copy(normed_h, normed, sems.at[0])
    caches = [
        pltpu.make_async_copy(kc_h.at[:, y], kc, sems.at[1]),
        pltpu.make_async_copy(vc_h.at[:, y], vc, sems.at[2]),
    ]
    for copy in [load] + caches:
        copy.start()
    stack = jnp.concatenate([b[640:656, :] for b in blocks], axis=0)
    upper = jnp.concatenate(
        [2.0 * mm(rank_order(ids, h, 0), stack) for h in range(2)], axis=1
    ).astype(BF)
    for n in range(8):
        row = ((x ^ ORDER[n // 2]) * 4 + c + n % 2 - 2 * c * (n % 2)) * 320
        for zh in range(2):
            to = pl.ds(pl.multiple_of(row + 640 * zh, 320), 320)
            lower[to, :] = blocks[n][zh * 320 : zh * 320 + 320, :]
    for n in range(10):
        rows = slice(n * 512, n * 512 + 512)
        merged[n] = (wq[rows, :].astype(F32) + mm(lower[rows, :], upper)).astype(BF)
    load.wait()
    total = mm(normed[0], merged[0])
    for n in range(1, 10):
        total = total + mm(normed[n], merged[n])
    qs[...] = total.astype(BF).astype(F32)
    for b in range(8):
        pieces_b = [
            qs[s * 64 + b * 8 : s * 64 + b * 8 + 8, h * 128 : h * 128 + 128] for s in range(4) for h in range(2)
        ]
        qa[b * 64 : b * 64 + 64, :] = jnp.concatenate(pieces_b, axis=0).astype(BF)
    for k, ref in enumerate(pieces):
        kv[(z ^ k) & 3] = ref[...]
    key_t = kv[0:2].reshape(128, 256)
    val = kv[2:4].reshape(128, 256).astype(F32).T.astype(BF)
    factor = 1.0 / HD**0.5
    sn_all[...] = mm(qa[...], key_t) * factor
    c8 = lax.broadcasted_iota(jnp.int32, (8, 512), 1)
    r8 = lax.broadcasted_iota(jnp.int32, (8, 512), 0)
    own_cached = (c8 >> 6) == r8
    pos = c8 & 63
    cn = lax.broadcasted_iota(jnp.int32, (64, 256), 1)
    rn = lax.broadcasted_iota(jnp.int32, (64, 256), 0)
    seen = (cn >> 6) <= (rn >> 4)

    for copy in caches:
        copy.wait()

    def batch(b, carry):
        r = pl.multiple_of(b * 8, 8)
        rows = pl.ds(pl.multiple_of(b * 64, 64), 64)
        keys = kc[pl.ds(r, 8)].reshape(512, 128)
        vals = vc[pl.ds(r, 8)].reshape(512, 128)
        length = jnp.zeros((8, 512), jnp.int32)
        for i in range(8):
            length = jnp.where(r8 == i, lens[r + i], length)
        ok = jnp.where(own_cached & (pos < length), 1.0, 0.0)
        okc = jnp.concatenate([ok] * 8, axis=0) > 0.5
        okn = seen & ((cn & 63) == (rn & 7) + r)
        sc = jnp.where(okc, mm_t(qa[rows, :], keys) * factor, -1e30)
        sn = jnp.where(okn, sn_all[rows, :], -1e30)
        top = jnp.max(jnp.maximum(fold(sc, jnp.maximum), fold(sn, jnp.maximum)), axis=1, keepdims=True)
        ec, en = jnp.exp(sc - top), jnp.exp(sn - top)
        total = jnp.sum(fold(ec, jnp.add) + fold(en, jnp.add), axis=1, keepdims=True)
        inverse = 1.0 / total
        pn_all[rows, :] = (en * inverse).astype(BF)
        oc[rows, :] = mm((ec * inverse).astype(BF), vals)
        return carry

    lax.fori_loop(0, 8, batch, 0, unroll=8)
    out = oc[...] + mm(pn_all[...], val)
    for b in range(8):
        for s in range(4):
            for h in range(2):
                n = b * 64 + (s * 2 + h) * 8
                qs[s * 64 + b * 8 : s * 64 + b * 8 + 8, h * 128 : h * 128 + 128] = out[n : n + 8]
    ctx[...] = qs[...].astype(BF)


def merge_o_kernel(ids, *refs):
    blocks = refs[:8]
    wo = refs[8]
    same, other = refs[9:12], refs[12:15]
    out, hold, low, own, sem = refs[15:]
    x, c, y, z = ids[0], ids[2], ids[3], ids[4]
    load = pltpu.make_async_copy(wo.at[:, pl.ds(pl.multiple_of(y * 1280, 1280), 1280)], own, sem)
    load.start()
    ks = x ^ y
    for k in range(4):
        for o in range(2):

            @pl.when(ks == k)
            def _():
                hold[o] = blocks[2 * ORDER[k] + o][0:640, :]

    order = [rank_order(ids, h, 64) for h in range(2)]
    for k in (1, 2, 3, 0):
        if k == 0:
            load.wait()
        yy = (y - k + 4) & 3
        at = pl.multiple_of(656 + 16 * yy, 16)
        stack = jnp.concatenate([b[pl.ds(at, 16), :] for b in blocks], axis=0)
        lower = jnp.concatenate([2.0 * mm(order[h], stack) for h in range(2)], axis=1)
        low[...] = lower.T.astype(BF)
        for zz in range(4):
            zh, cc = zz // 2, zz % 2
            o = c + cc - 2 * c * cc
            u = hold[o, zh * 320 : zh * 320 + 320, :]
            cols = slice(zz * 320, zz * 320 + 320)
            if k == 0:
                out[k, zz ^ z] = (own[:, cols].astype(F32) + mm_t(low[...], u)).astype(BF)
            else:
                for ref, core in ((same[k - 1], c), (other[k - 1], 1 - c)):
                    at = pl.ds(pl.multiple_of(core * 128, 128), 128)
                    out[k, zz ^ z, at] = (ref[:, cols].astype(F32) + mm_t(low[at, :], u)).astype(BF)


def begin_kernel(c0, c1, merged, out):
    for n in range(4):
        out[n] = mm(c0[...], merged[0, n]) + mm(c1[...], merged[1, n])


def project_kernel(order, c3, c2, merged, begun, *out):
    for n, ref_out in zip(order, out):
        total = begun[n] + mm(c3[...], merged[3, n]) + mm(c2[...], merged[2, n])
        total = total.astype(BF)
        ref_out[0:256] = total[:, 0:128]
        ref_out[256:512] = total[:, 128:256]
        ref_out[512:640] = jnp.concatenate([total[0:128, 256:320], total[128:256, 256:320]], axis=1)


def sum_kernel(p0, p1, p2, p3, out):
    total = p0[...].astype(F32) + p1[...].astype(F32) + p2[...].astype(F32) + p3[...].astype(F32)
    tail = jnp.concatenate([total[512:640, :64], total[512:640, 64:]], axis=0)
    full = jnp.concatenate([total[0:256], total[256:512], tail], axis=1).astype(BF)
    out[...] = full.reshape(out.shape)


def near(a):
    return pltpu.with_memory_space_constraint(a, pltpu.VMEM)


def far(a):
    return pltpu.with_memory_space_constraint(a, pltpu.HBM)


def ring(s):
    return [(i, (i + s) % 4) for i in range(4)]


def partner(s):
    return [(i, i ^ s) for i in range(4)]


def kv_pairs(k):
    pairs = []
    for s in range(16):
        a, e, b = s // 4, (s % 4) // 2, s % 2
        pairs.append((s, (2 * (a % 2) + e) * 4 + (((a // 2) * 2 + b) ^ k)))
    return pairs


def local(states, wq, wkv, wo, qa_low, qa_up, oa_low, oa_up, kcache, vcache, lens):
    x, zh, c, y, z = (lax.axis_index(a) for a in ("x", "zh", "c", "y", "z"))
    ids = jnp.stack([x, zh, c, y, z]).astype(jnp.int32)

    vmem = pl.BlockSpec(memory_space=pltpu.VMEM)
    hbm = pl.BlockSpec(memory_space=pltpu.HBM)

    def array(*shape):
        return jax.ShapeDtypeStruct(shape, BF)

    messages = pl.pallas_call(
        pack_kernel,
        out_shape=array(32, MSG, 128),
        compiler_params=params(4),
        name="pack",
    )(*(far(a) for a in (qa_low, oa_up, qa_up, oa_low)))
    got = lax.all_to_all(messages, ("zh", "y", "z"), 0, 0, tiled=True)

    normed, kv_t, *w_sent = pl.pallas_call(
        norm_kernel,
        out_shape=(pltpu.HBM((10, ROWS, 512), BF), array(64, ROWS)) + (pltpu.HBM((128, 1280), BF),) * 3,
        in_specs=[SMEM, hbm, hbm, hbm],
        out_specs=(hbm, vmem, hbm, hbm, hbm),
        scratch_shapes=[
            pltpu.VMEM((STEPS, 64, WIDTH), BF),
            pltpu.VMEM((64, WIDTH), BF),
            pltpu.VMEM((10, ROWS, 512), BF),
            pltpu.VMEM((3, 128, 1280), BF),
            pltpu.SemaphoreType.DMA((15,)),
        ],
        compiler_params=params(20),
        cost_estimate=pl.CostEstimate(flops=170_000_000, bytes_accessed=8_000_000, transcendentals=0),
        name="norm_kv",
    )(ids, far(states), far(wkv.T), far(wo))

    new_kv = [lax.ppermute(kv_t, TP, kv_pairs(k)) for k in range(4)]

    swap = [(0, 1), (1, 0)]
    got, normed, kv_t = lax.optimization_barrier((got, normed, kv_t))
    mine = pl.pallas_call(
        sort_kernel,
        out_shape=array(XROWS, 128),
        in_specs=[SMEM, vmem],
        compiler_params=params(6),
        name="sort_rows",
    )(ids, got)
    mine, w_sent, new_kv = lax.optimization_barrier((mine, w_sent, new_kv))
    w_first = lax.ppermute(w_sent[0], "y", ring(1))
    w_third = lax.ppermute(w_sent[2], "y", ring(3))
    parts = [mine] + [lax.ppermute(mine, "x", partner(s)) for s in ORDER[1:]]
    w_first, w_third, w_second = lax.optimization_barrier((w_first, w_third, w_sent[1]))
    w_same = [w_first, lax.ppermute(w_second, "y", ring(2)), w_third]
    blocks = []
    for part in parts:
        blocks += [part, lax.ppermute(part, "c", swap)]

    ctx = pl.pallas_call(
        attend_kernel,
        out_shape=array(ROWS, 256),
        in_specs=[SMEM] + [vmem] * 9 + [hbm] * 3 + [vmem] * 4 + [SMEM],
        scratch_shapes=[
            pltpu.VMEM((4, 64, 256), BF),
            pltpu.VMEM((ROWS, 256), F32),
            pltpu.VMEM((512, 128), BF),
            pltpu.VMEM((512, 256), F32),
            pltpu.VMEM((512, 256), BF),
            pltpu.VMEM((512, 128), F32),
            pltpu.VMEM((10, ROWS, 512), BF),
            pltpu.VMEM((WIDTH, 128), BF),
            pltpu.VMEM((10, 512, 256), BF),
            pltpu.VMEM((64, 64, 128), BF),
            pltpu.VMEM((64, 64, 128), BF),
            pltpu.SemaphoreType.DMA((3,)),
        ],
        compiler_params=params(24),
        cost_estimate=pl.CostEstimate(flops=1_000_000_000, bytes_accessed=10_000_000, transcendentals=400_000),
        name="attend",
    )(ids, *blocks, near(wq), far(normed), far(kcache), far(vcache), *new_kv, lens)

    others = {s: lax.ppermute(ctx, "y", ring(s)) for s in (1, 3, 2)}
    _, w_same = lax.optimization_barrier((ctx, w_same))
    w_other = [lax.ppermute(w, "c", swap) for w in w_same]
    merged = pl.pallas_call(
        merge_o_kernel,
        out_shape=array(4, 4, 256, 320),
        in_specs=[SMEM] + [vmem] * 8 + [hbm] + [vmem] * 6,
        scratch_shapes=[
            pltpu.VMEM((2, 640, 128), BF),
            pltpu.VMEM((256, 128), BF),
            pltpu.VMEM((256, 1280), BF),
            pltpu.SemaphoreType.DMA(()),
        ],
        compiler_params=params(20),
        cost_estimate=pl.CostEstimate(flops=340_000_000, bytes_accessed=8_000_000, transcendentals=0),
        name="merge_o",
    )(ids, *blocks, far(wo), *w_same, *w_other)
    begun = pl.pallas_call(
        begin_kernel,
        out_shape=jax.ShapeDtypeStruct((4, ROWS, 320), F32),
        compiler_params=params(16),
        cost_estimate=pl.CostEstimate(flops=340_000_000, bytes_accessed=4_000_000, transcendentals=0),
        name="begin",
    )(ctx, others[1], merged)
    sums = {}
    for order in ((2,), (1,), (3, 0)):
        both = pl.pallas_call(
            functools.partial(project_kernel, order),
            out_shape=(array(640, 128),) * len(order),
            compiler_params=params(16),
            cost_estimate=pl.CostEstimate(flops=340_000_000, bytes_accessed=4_000_000, transcendentals=0),
            name="project",
        )(others[3], others[2], merged, begun)
        sums.update(zip(order, both))
    came = [lax.ppermute(sums[n], "z", partner(n)) for n in (2, 1, 3)]
    return pl.pallas_call(
        sum_kernel,
        out_shape=array(4, 64, 320),
        compiler_params=params(6),
        name="sum_parts",
    )(sums[0], *came)


def solution(mesh):
    fine = Mesh(np.asarray(mesh.devices).reshape(NX, NZH, NC, NY, NZ), GROUP + TP)
    every = GROUP + TP
    in_specs = (
        P(None, GROUP, None),
        P(None, TP),
        P(None, TP),
        P(TP, None),
        P(every, None),
        P(GROUP, TP),
        P(GROUP, TP),
        P(every, None),
        P(GROUP, None, None, None),
        P(GROUP, None, None, None),
        P(GROUP),
    )
    out_specs = P(None, GROUP, TP)
    return jax.shard_map(local, mesh=fine, in_specs=in_specs, out_specs=out_specs, check_vma=False)
```
